32 devices in a mesh: narrow: 8 (over z, core), wide: 4 (over y, x).
Axes of the slice: x: 2, y: 2, z: 4, core: 2. Of those that a mesh axis runs over, the one named last changes fastest.
Arguments:
- inputs: bfloat16 [1024, 8192], P('narrow', 'wide'), may hold values from -6 to 6
- gate_blocks: bfloat16 [112, 16, 128, 128], P('wide', 'narrow'), may hold values from -0.125 to 0.125
- up_blocks: bfloat16 [112, 16, 128, 128], P('wide', 'narrow'), may hold values from -0.125 to 0.125
- pattern: int32 [112, 16], P('wide'), may hold values from 0 to 63, as said below
- grad_hidden: bfloat16 [1024, 14336], P('narrow', 'wide'), may hold values from -0.59765625 to 0.59765625
Outputs:
- hidden: bfloat16 [1024, 14336], P('narrow', 'wide')
- grad_inputs: bfloat16 [1024, 8192], P('narrow', 'wide')
- grad_gate: bfloat16 [112, 16, 128, 128], P('wide', 'narrow')
- grad_up: bfloat16 [112, 16, 128, 128], P('wide', 'narrow')
The draws below stay inside these ranges and needn't reach their ends.
Inputs may be any that keep to these rules, and one draw needn't show every extreme that they name: pattern[j, k] = b_j XOR m_k, with one offset b_j for each block column and 16 distinct masks m_k common to all block columns, so each block column lists 16 distinct block rows.
All inputs are finite; a program needn't handle non-finite values.
Results may differ from the reference program's by a relative error of at most 0.023.
Values may be sent and summed in bfloat16 or wider, within the bound.
No kernel may reach another device: no remote copies, remote signals or barrier semaphores. Data moves between devices by JAX's collectives and lax.ppermute only.
A program may use at most 192 MiB of HBM per device.

```python
import jax
import jax.numpy as jnp
from jax import lax

D = 8192
FF = 14336
BLK = 128
TOK_DEV = 128
FB = 112
NZ = 16
TOKENS = 1024
N_NARROW = 8
N_WIDE = 4


def draw_pattern(key, part):
    row_blocks = D // BLK
    slots = row_blocks // 4
    columns = FF // BLK
    key_rank, key_base = jax.random.split(key)
    ranking = jax.random.permutation(key_rank, row_blocks).astype(jnp.int32)
    numbers = jnp.arange(row_blocks, dtype=jnp.int32)
    butterfly = jnp.bitwise_and(numbers, numbers - 1) == 0
    scores = jnp.where(butterfly, ranking, row_blocks + ranking)
    masks = jnp.argsort(scores)[:slots].astype(jnp.int32)
    offset = jax.random.randint(key_base, (), 0, row_blocks, dtype=jnp.int32)
    column_base = jnp.bitwise_xor(jnp.arange(columns, dtype=jnp.int32) % row_blocks, offset)
    return jnp.bitwise_xor(column_base[:, None], masks[None, :]).astype(jnp.int32)


def levels(own_key, shape, cuts, least, high):
    def one(position, shards_of):
        draws = jax.random.uniform(jax.random.fold_in(jax.random.fold_in(own_key, 6), position), (shards_of,), jnp.float32, least / len(cuts), high / len(cuts))
        return jnp.repeat(jnp.exp(draws), shape[position] // shards_of).reshape((-1,) + (1,) * (len(shape) - position - 1))

    level = one(*cuts[0])
    for cut in cuts[1:]:
        level = level * one(*cut)
    return level


def bell_draw(stream_key, extent, scale, reach, cuts=(), kind=jnp.bfloat16):
    loudness = levels(stream_key, extent, cuts, -0.22, 0.18) if cuts else 1.0
    values = jax.random.normal(stream_key, extent, jnp.float32) * scale * loudness
    return jnp.minimum(jnp.maximum(values, -reach), reach).astype(kind)


def setup_inputs(seed: int = 0) -> dict:
    splits = jax.random.split(jax.random.key(seed), 6)
    return {
        "inputs": bell_draw(splits[0], (TOKENS, D), 1.0, 6.0, ((0, 8), (1, 4))),
        "gate_blocks": bell_draw(splits[1], (FB, NZ, BLK, BLK), (NZ * BLK) ** -0.5, 0.125, ((0, 4), (1, 8))),
        "up_blocks": bell_draw(splits[2], (FB, NZ, BLK, BLK), (NZ * BLK) ** -0.5, 0.125, ((0, 4), (1, 8))),
        "pattern": draw_pattern(jax.random.fold_in(splits[5], 71), 0),
        "grad_hidden": bell_draw(splits[4], (TOKENS, FF), 0.1, 0.59765625, ((0, 8), (1, 4))),
    }


def silu_parts(gate_sum):
    sigmoid_value = jax.nn.sigmoid(gate_sum)
    return gate_sum * sigmoid_value, sigmoid_value * (1.0 + gate_sum * (1.0 - sigmoid_value))


def rounded(values):
    return lax.optimization_barrier(values.astype(jnp.bfloat16)).astype(jnp.float32)


def reference(inputs, gate_blocks, up_blocks, pattern, grad_hidden):
    row_blocks = D // BLK
    columns = FF // BLK
    slots = row_blocks // 4
    group_columns = columns // N_WIDE
    token_groups = inputs.reshape(N_NARROW, TOK_DEV, row_blocks, BLK)
    cotangent_groups = grad_hidden.reshape(N_NARROW, TOK_DEV, columns, BLK)
    gate_weights = gate_blocks.astype(jnp.float32)
    up_weights = up_blocks.astype(jnp.float32)
    wide_ids = jnp.arange(N_WIDE, dtype=jnp.int32)[:, None, None]
    wide_pattern = pattern.reshape(N_WIDE, group_columns, slots)

    def one_group(totals, group_item):
        group_inputs, group_cotangent = group_item
        picked = group_inputs[:, pattern].astype(jnp.float32)
        gate_sum = jnp.einsum('tjkb,jkbc->tjc', picked, gate_weights)
        up_sum = jnp.einsum('tjkb,jkbc->tjc', picked, up_weights)
        activation, derivative = silu_parts(gate_sum)
        hidden = (activation * up_sum).astype(jnp.bfloat16)
        cotangent = group_cotangent.astype(jnp.float32)
        d_gate = rounded(cotangent * up_sum * derivative)
        d_up = rounded(cotangent * activation)
        contribution = jnp.einsum('tjc,jkbc->tjkb', d_gate, gate_weights) + jnp.einsum('tjc,jkbc->tjkb', d_up, up_weights)
        shaped = contribution.reshape(TOK_DEV, N_WIDE, group_columns, slots, BLK).transpose(1, 2, 3, 0, 4)
        scattered = jnp.zeros((N_WIDE, row_blocks, TOK_DEV, BLK), jnp.float32).at[wide_ids, wide_pattern].add(shaped)
        grad_group = jnp.sum(rounded(scattered), axis=0).transpose(1, 0, 2).reshape(TOK_DEV, D).astype(jnp.bfloat16)
        gate_term = rounded(jnp.einsum('tjkb,tjc->jkbc', picked, d_gate))
        up_term = rounded(jnp.einsum('tjkb,tjc->jkbc', picked, d_up))
        return (totals[0] + gate_term, totals[1] + up_term), (hidden.reshape(TOK_DEV, FF), grad_group)

    zero_grads = jnp.zeros((columns, slots, BLK, BLK), jnp.float32)
    totals, outputs = lax.scan(one_group, (zero_grads, zero_grads), (token_groups, cotangent_groups))
    hiddens, grads = outputs
    return (hiddens.reshape(TOKENS, FF), grads.reshape(TOKENS, D), totals[0].astype(jnp.bfloat16), totals[1].astype(jnp.bfloat16))
```

```python
import functools

import jax
import jax.numpy as jnp
from jax import lax
from jax.experimental import pallas as pl
from jax.experimental.pallas import tpu as pltpu
from jax.sharding import PartitionSpec as P


def silu_parts(gate_sum):
    sigmoid_value = jax.nn.sigmoid(gate_sum)
    return (gate_sum * sigmoid_value, sigmoid_value * (1.0 + gate_sum * (1.0 - sigmoid_value)))


def gathered_weights(inputs, gate_blocks, up_blocks, pattern, grad_hidden):
    tokens_here = inputs.shape[0]
    block_size = gate_blocks.shape[2]
    columns = gate_blocks.shape[0]
    full_inputs = lax.all_gather(inputs, "wide", axis=1, tiled=True)
    row_blocks = full_inputs.shape[1] // block_size
    input_blocks = full_inputs.reshape(tokens_here, row_blocks, block_size)
    picked = jnp.take(input_blocks, pattern, axis=1)
    gate_all = lax.all_gather(gate_blocks, "narrow", axis=1, tiled=True)
    up_all = lax.all_gather(up_blocks, "narrow", axis=1, tiled=True)
    gate_sum = jnp.einsum("tjkb,jkbc->tjc", picked, gate_all, preferred_element_type=jnp.float32)
    up_sum = jnp.einsum("tjkb,jkbc->tjc", picked, up_all, preferred_element_type=jnp.float32)
    activation, derivative = silu_parts(gate_sum)
    hidden = (activation * up_sum).astype(jnp.bfloat16)
    cotangent = grad_hidden.reshape(tokens_here, columns, block_size).astype(jnp.float32)
    d_gate = (cotangent * up_sum * derivative).astype(jnp.bfloat16)
    d_up = (cotangent * activation).astype(jnp.bfloat16)
    zero_inputs = jnp.zeros((tokens_here, row_blocks, block_size), jnp.float32)

    def one_slot(k, running):
        gate_slot = lax.dynamic_index_in_dim(gate_all, k, 1, keepdims=False)
        up_slot = lax.dynamic_index_in_dim(up_all, k, 1, keepdims=False)
        contribution = jnp.einsum(
            "tjc,jbc->tjb", d_gate, gate_slot, preferred_element_type=jnp.float32
        )
        contribution = contribution + jnp.einsum(
            "tjc,jbc->tjb", d_up, up_slot, preferred_element_type=jnp.float32
        )
        targets = lax.dynamic_index_in_dim(pattern, k, 1, keepdims=False)
        return running.at[:, targets].add(contribution)

    partial_inputs = lax.fori_loop(0, gate_all.shape[1], one_slot, zero_inputs)
    grad_inputs = lax.psum_scatter(
        partial_inputs.reshape(tokens_here, row_blocks * block_size).astype(jnp.bfloat16),
        "wide",
        scatter_dimension=1,
        tiled=True,
    )
    gate_terms = jnp.einsum("tjkb,tjc->jkbc", picked, d_gate, preferred_element_type=jnp.float32)
    up_terms = jnp.einsum("tjkb,tjc->jkbc", picked, d_up, preferred_element_type=jnp.float32)
    grad_gate = lax.psum_scatter(
        gate_terms.astype(jnp.bfloat16), "narrow", scatter_dimension=1, tiled=True
    )
    grad_up = lax.psum_scatter(
        up_terms.astype(jnp.bfloat16), "narrow", scatter_dimension=1, tiled=True
    )
    return hidden.reshape(tokens_here, columns * block_size), grad_inputs, grad_gate, grad_up


def column_kernel(nz, nw, spd, places, *refs):
    refs = list(refs)

    def take(n):
        out = refs[:n]
        del refs[:n]
        return out

    x_in = take(nz * nw)
    w_in = take(nz * 2)
    gh_in = take(nz)
    hid_out = take(nz)
    dw_out = take(nz * 2)
    dx_out = take(nw)
    x_all, dx_all, x_col, w_col, d_col, sems = refs
    step = pl.program_id(0)
    tokens = x_in[0].shape[0]
    blk = w_in[0].shape[-1]
    slots = nz * 2 * spd

    @pl.when(step == 0)
    def _():
        copies = [
            pltpu.make_async_copy(
                x_in[r * nw + m], x_all.at[m, pl.ds(r * tokens, tokens)], sems.at[r * nw + m]
            )
            for r in range(nz)
            for m in range(nw)
        ]
        for c in copies:
            c.start()
        dx_all[...] = jnp.zeros_like(dx_all)
        for c in copies:
            c.wait()

    def place(q):
        return places[step, q, 0], pl.multiple_of(places[step, q, 1] * blk, blk)

    for q in range(slots):
        piece = w_in[q // spd]
        m, at = place(q)
        x_col[:, q * blk : (q + 1) * blk] = x_all[m, :, pl.ds(at, blk)]
        w_col[q * blk : (q + 1) * blk, :blk] = piece[0, 0, q % spd]
        w_col[q * blk : (q + 1) * blk, blk:] = piece[1, 0, q % spd]
    both = jnp.dot(x_col[...], w_col[...], preferred_element_type=jnp.float32)
    gate, up = both[:, :blk], both[:, blk:]
    activation, derivative = silu_parts(gate)
    hidden = (activation * up).astype(jnp.bfloat16)
    cotangent = jnp.concatenate([g[...] for g in gh_in], axis=0).astype(jnp.float32)
    d_col[:, :blk] = (cotangent * up * derivative).astype(jnp.bfloat16)
    d_col[:, blk:] = (cotangent * activation).astype(jnp.bfloat16)
    for r in range(nz):
        hid_out[r][...] = hidden[r * tokens : (r + 1) * tokens]
    for p in range(slots // 2):
        span = slice(2 * p * blk, (2 * p + 2) * blk)
        grads = lax.dot_general(
            x_col[:, span], d_col[...], (((0,), (0,)), ((), ())), preferred_element_type=jnp.float32
        ).astype(jnp.bfloat16)
        share = lax.dot_general(
            d_col[...], w_col[span], (((1,), (1,)), ((), ())), preferred_element_type=jnp.float32
        )
        for h in range(2):
            q = 2 * p + h
            rows = grads[h * blk : (h + 1) * blk]
            dw_out[q // spd][0, 0, q % spd] = rows[:, :blk]
            dw_out[q // spd][1, 0, q % spd] = rows[:, blk:]
            m, at = place(q)
            dx_all[m, :, pl.ds(at, blk)] += share[:, h * blk : (h + 1) * blk]

    @pl.when(step == pl.num_programs(0) - 1)
    def _():
        for m in range(nw):
            dx_out[m][...] = dx_all[m].astype(jnp.bfloat16)


def columns_call(nz, nw, places, x_parts, w_parts, gh_parts):
    tokens, features = x_parts[0].shape
    _, cols, spd, blk, _ = w_parts[0].shape
    rows = nz * tokens
    slots = nz * 2 * spd
    bf = jnp.bfloat16
    w_spec = pl.BlockSpec((2, 1, spd, blk, blk), lambda j, s: (0, j, 0, 0, 0))
    h_spec = pl.BlockSpec((tokens, blk), lambda j, s: (0, j))
    dx_spec = pl.BlockSpec((rows, features), lambda j, s: (0, 0), pipeline_mode=pl.Buffered(1))
    flops = 3 * 2 * rows * slots * blk * 2 * blk * cols
    return pl.pallas_call(
        functools.partial(column_kernel, nz, nw, spd),
        grid_spec=pltpu.PrefetchScalarGridSpec(
            num_scalar_prefetch=1,
            grid=(cols,),
            in_specs=[pl.BlockSpec(memory_space=pl.ANY)] * (nz * nw)
            + [w_spec] * (nz * 2)
            + [h_spec] * nz,
            out_specs=[h_spec] * nz + [w_spec] * (nz * 2) + [dx_spec] * nw,
            scratch_shapes=[
                pltpu.VMEM((nw, rows, features), bf),
                pltpu.VMEM((nw, rows, features), jnp.float32),
                pltpu.VMEM((rows, slots * blk), bf),
                pltpu.VMEM((slots * blk, 2 * blk), bf),
                pltpu.VMEM((rows, 2 * blk), bf),
                pltpu.SemaphoreType.DMA((nz * nw,)),
            ],
        ),
        out_shape=[jax.ShapeDtypeStruct((tokens, cols * blk), bf)] * nz
        + [jax.ShapeDtypeStruct(w_parts[0].shape, bf)] * (nz * 2)
        + [jax.ShapeDtypeStruct((rows, features), bf)] * nw,
        compiler_params=pltpu.CompilerParams(
            dimension_semantics=("arbitrary",), vmem_limit_bytes=58 * 1024 * 1024
        ),
        cost_estimate=pl.CostEstimate(flops=flops, bytes_accessed=40_000_000, transcendentals=0),
    )(places, *x_parts, *w_parts, *gh_parts)


def moved_tokens(narrow, nw, inputs, gate_blocks, up_blocks, pattern, grad_hidden):
    nz = narrow // 2
    tokens = inputs.shape[0]
    features = inputs.shape[1]
    all_cols, spd, blk, _ = gate_blocks.shape
    cols = all_cols // nz
    width = cols * blk
    me = lax.axis_index("narrow")
    z, core = me // 2, me % 2
    wide = lax.axis_index("wide")

    def along_z(a, s):
        return lax.ppermute(a, "narrow", [(i, (i + 2 * s) % narrow) for i in range(narrow)])

    def swap(a):
        return lax.ppermute(a, "narrow", [(i, i ^ 1) for i in range(narrow)])

    def over_wide(a, m):
        return lax.ppermute(a, "wide", [(i, i ^ m) for i in range(nw)])

    def ahead(r):
        return lax.rem(z + r, nz)

    mine = lax.dynamic_slice_in_dim(pattern, cols * z, cols, 0)
    slot_of = jnp.stack(
        [
            ((z - r + nz) % nz * 2 + (core ^ c)) * spd + i
            for r in range(nz)
            for c in range(2)
            for i in range(spd)
        ]
    )
    rows_of = jnp.take(mine, slot_of, axis=1)
    per_device = features // blk
    places = jnp.stack([(rows_of // per_device) ^ wide, rows_of % per_device], axis=-1)

    x_z = [inputs] + [along_z(inputs, r) for r in range(1, nz)]
    x_parts = []
    for r in range(nz):
        x_parts += [x_z[r]] + [over_wide(x_z[r], m) for m in range(1, nw)]

    w_parts = []
    for r in range(nz):
        piece = jnp.stack(
            [
                lax.dynamic_slice_in_dim(a, cols * ahead(r), cols, 0)
                for a in (gate_blocks, up_blocks)
            ]
        )
        if r:
            piece = along_z(piece, r)
        w_parts += [piece, swap(piece)]
    gh_parts = []
    for r in range(nz):
        piece = lax.dynamic_slice_in_dim(grad_hidden, width * ahead(r), width, 1)
        gh_parts.append(along_z(piece, r) if r else piece)

    outs = columns_call(nz, nw, places, x_parts, w_parts, gh_parts)
    hid, dw, dx = outs[:nz], outs[nz : 3 * nz], outs[3 * nz :]

    f32 = jnp.float32
    total = dx[0].astype(f32)
    for m in range(1, nw):
        total = total + over_wide(dx[m], m).astype(f32)
    total = total.astype(jnp.bfloat16).reshape(nz, tokens, features)
    back = total[0].astype(f32)
    for r in range(1, nz):
        back = back + along_z(total[r], nz - r).astype(f32)
    grad_inputs = back.astype(jnp.bfloat16)

    hidden = jnp.zeros((tokens, nz * width), jnp.bfloat16)
    grad_gate = jnp.zeros(gate_blocks.shape, jnp.bfloat16)
    grad_up = jnp.zeros(gate_blocks.shape, jnp.bfloat16)
    for r in range(nz):
        h = along_z(hid[r], nz - r) if r else hid[r]
        hidden = lax.dynamic_update_slice_in_dim(hidden, h, width * ahead(r), 1)
        both = (dw[2 * r].astype(f32) + swap(dw[2 * r + 1]).astype(f32)).astype(jnp.bfloat16)
        if r:
            both = along_z(both, nz - r)
        grad_gate = lax.dynamic_update_slice_in_dim(grad_gate, both[0], cols * ahead(r), 0)
        grad_up = lax.dynamic_update_slice_in_dim(grad_up, both[1], cols * ahead(r), 0)
    return hidden, grad_inputs, grad_gate, grad_up


def solution(mesh):
    narrow, nw = mesh.shape["narrow"], mesh.shape["wide"]

    def shards(inputs, gate_blocks, up_blocks, pattern, grad_hidden):
        columns = gate_blocks.shape[0]
        if narrow % 2 == 0 and columns % (narrow // 2) == 0 and nw & (nw - 1) == 0:
            return moved_tokens(
                narrow, nw, inputs, gate_blocks, up_blocks, pattern, grad_hidden
            )
        return gathered_weights(inputs, gate_blocks, up_blocks, pattern, grad_hidden)

    placed = (
        P("narrow", "wide"),
        P("wide", "narrow", None, None),
        P("wide", "narrow", None, None),
        P("wide", None),
        P("narrow", "wide"),
    )
    return jax.shard_map(
        shards,
        mesh=mesh,
        in_specs=placed,
        out_specs=(
            P("narrow", "wide"),
            P("narrow", "wide"),
            P("wide", "narrow", None, None),
            P("wide", "narrow", None, None),
        ),
        check_vma=False,
    )
```

```python
import functools

import jax
import jax.numpy as jnp
from jax import lax
from jax.experimental import pallas as pl
from jax.experimental.pallas import tpu as pltpu
from jax.sharding import PartitionSpec as P


def silu_parts(gate_sum):
    sigmoid_value = jax.nn.sigmoid(gate_sum)
    return (gate_sum * sigmoid_value, sigmoid_value * (1.0 + gate_sum * (1.0 - sigmoid_value)))


def gathered_weights(inputs, gate_blocks, up_blocks, pattern, grad_hidden):
    tokens_here = inputs.shape[0]
    block_size = gate_blocks.shape[2]
    columns = gate_blocks.shape[0]
    full_inputs = lax.all_gather(inputs, "wide", axis=1, tiled=True)
    row_blocks = full_inputs.shape[1] // block_size
    input_blocks = full_inputs.reshape(tokens_here, row_blocks, block_size)
    picked = jnp.take(input_blocks, pattern, axis=1)
    gate_all = lax.all_gather(gate_blocks, "narrow", axis=1, tiled=True)
    up_all = lax.all_gather(up_blocks, "narrow", axis=1, tiled=True)
    gate_sum = jnp.einsum("tjkb,jkbc->tjc", picked, gate_all, preferred_element_type=jnp.float32)
    up_sum = jnp.einsum("tjkb,jkbc->tjc", picked, up_all, preferred_element_type=jnp.float32)
    activation, derivative = silu_parts(gate_sum)
    hidden = (activation * up_sum).astype(jnp.bfloat16)
    cotangent = grad_hidden.reshape(tokens_here, columns, block_size).astype(jnp.float32)
    d_gate = (cotangent * up_sum * derivative).astype(jnp.bfloat16)
    d_up = (cotangent * activation).astype(jnp.bfloat16)
    zero_inputs = jnp.zeros((tokens_here, row_blocks, block_size), jnp.float32)

    def one_slot(k, running):
        gate_slot = lax.dynamic_index_in_dim(gate_all, k, 1, keepdims=False)
        up_slot = lax.dynamic_index_in_dim(up_all, k, 1, keepdims=False)
        contribution = jnp.einsum(
            "tjc,jbc->tjb", d_gate, gate_slot, preferred_element_type=jnp.float32
        )
        contribution = contribution + jnp.einsum(
            "tjc,jbc->tjb", d_up, up_slot, preferred_element_type=jnp.float32
        )
        targets = lax.dynamic_index_in_dim(pattern, k, 1, keepdims=False)
        return running.at[:, targets].add(contribution)

    partial_inputs = lax.fori_loop(0, gate_all.shape[1], one_slot, zero_inputs)
    grad_inputs = lax.psum_scatter(
        partial_inputs.reshape(tokens_here, row_blocks * block_size).astype(jnp.bfloat16),
        "wide",
        scatter_dimension=1,
        tiled=True,
    )
    gate_terms = jnp.einsum("tjkb,tjc->jkbc", picked, d_gate, preferred_element_type=jnp.float32)
    up_terms = jnp.einsum("tjkb,tjc->jkbc", picked, d_up, preferred_element_type=jnp.float32)
    grad_gate = lax.psum_scatter(
        gate_terms.astype(jnp.bfloat16), "narrow", scatter_dimension=1, tiled=True
    )
    grad_up = lax.psum_scatter(
        up_terms.astype(jnp.bfloat16), "narrow", scatter_dimension=1, tiled=True
    )
    return hidden.reshape(tokens_here, columns * block_size), grad_inputs, grad_gate, grad_up


BF16, F32 = jnp.bfloat16, jnp.float32
CHUNKS = 2


ANY = pl.BlockSpec(memory_space=pl.ANY)


def taker(refs):
    refs = list(refs)

    def take(n):
        out = refs[:n]
        del refs[:n]
        return out

    return take


def place_of(places, step, q, blk):
    return places[step, q, 0], pl.multiple_of(places[step, q, 1] * blk, blk)


def forward_kernel(nz, nw, spd, unread, layout, places, *refs):
    take = taker(refs)
    x_in = take(len(layout))
    w_own, w_other = take(nz), take(nz)
    take(unread)
    (g_own, g_other, d_out) = take(nz), take(1)[0], take(1)[0]
    x_all, x_col, w_col, sems = take(4)
    step = pl.program_id(0)
    tokens = d_out.shape[1] // nz
    blk = d_out.shape[-1] // 2
    slots = nz * 2 * spd

    @pl.when(step == 0)
    def _():
        copies = []
        for source, pieces in zip(x_in, layout):
            for at, m, rows, n in pieces:
                target = x_all.at[m, pl.ds(rows, n)]
                sem = sems.at[len(copies)]
                copies.append(pltpu.make_async_copy(source.at[pl.ds(at, n)], target, sem))
        for c in copies:
            c.start()
        for c in copies:
            c.wait()

    for q in range(slots):
        r, i = q // (2 * spd), q % spd
        piece = (w_other if q // spd % 2 else w_own)[r]
        m, at = place_of(places, step, q, blk)
        x_col[:, q * blk : (q + 1) * blk] = x_all[m, :, pl.ds(at, blk)]
        w_col[q * blk : (q + 1) * blk, :blk] = piece[i, 0]
        w_col[q * blk : (q + 1) * blk, blk:] = piece[spd + i, 0]
    both = jnp.dot(x_col[...], w_col[...], preferred_element_type=F32)
    gate, up = both[:, :blk], both[:, blk:]
    activation, derivative = silu_parts(gate)
    hidden = (activation * up).astype(BF16)
    cotangent = jnp.concatenate([w[2 * spd, 0] for w in w_own], axis=0).astype(F32)
    d_out[0, :, :blk] = (cotangent * up * derivative).astype(BF16)
    d_out[0, :, blk:] = (cotangent * activation).astype(BF16)
    for r in range(nz):
        g_own[r][2 * spd, 0] = hidden[r * tokens : (r + 1) * tokens]
        g_other[r, 2 * spd, 0] = jnp.zeros((tokens, blk), BF16)
    for p in range(slots // 2):
        grads = lax.dot_general(
            x_col[:, 2 * p * blk : (2 * p + 2) * blk],
            d_out[0],
            (((0,), (0,)), ((), ())),
            preferred_element_type=F32,
        ).astype(BF16)
        for h in range(2):
            q = 2 * p + h
            r, i = q // (2 * spd), q % spd
            rows = grads[h * blk : (h + 1) * blk]
            target = g_other.at[r] if q // spd % 2 else g_own[r]
            target[i, 0] = rows[:, :blk]
            target[spd + i, 0] = rows[:, blk:]


def forward_call(lo, nw, tokens, places, layout, x_parts, w_own, w_other, earlier):
    nz, features = len(w_own), x_parts[0].shape[1]
    parts, cols, blk, _ = w_own[1].shape
    spd = parts // 2
    rows, slots = nz * tokens, nz * 2 * spd
    own = pl.BlockSpec((parts, 1, blk, blk), lambda j, s: (0, j, 0, 0))
    own0 = pl.BlockSpec((parts, 1, blk, blk), lambda j, s: (0, j + lo, 0, 0))
    other = pl.BlockSpec((2 * spd, 1, blk, blk), lambda j, s: (0, j, 0, 0))
    other0 = pl.BlockSpec((2 * spd, 1, blk, blk), lambda j, s: (0, j + lo, 0, 0))
    every = pl.BlockSpec((nz, parts, 1, blk, blk), lambda j, s: (0, 0, j, 0, 0))
    d_spec = pl.BlockSpec((1, rows, 2 * blk), lambda j, s: (j, 0, 0))
    outs = pl.pallas_call(
        functools.partial(forward_kernel, nz, nw, spd, len(earlier), layout),
        grid_spec=pltpu.PrefetchScalarGridSpec(
            num_scalar_prefetch=1,
            grid=(cols,),
            in_specs=[ANY] * len(x_parts)
            + [own0]
            + [own] * (nz - 1)
            + [other0]
            + [other] * (nz - 1)
            + [ANY] * len(earlier),
            out_specs=[own] * nz + [every, d_spec],
            scratch_shapes=[
                pltpu.VMEM((nw, rows, features), BF16),
                pltpu.VMEM((rows, slots * blk), BF16),
                pltpu.VMEM((slots * blk, 2 * blk), BF16),
                pltpu.SemaphoreType.DMA((sum(len(p) for p in layout),)),
            ],
        ),
        out_shape=[jax.ShapeDtypeStruct(w_own[1].shape, BF16)] * nz
        + [
            jax.ShapeDtypeStruct((nz, *w_own[1].shape), BF16),
            jax.ShapeDtypeStruct((cols, rows, 2 * blk), BF16),
        ],
        compiler_params=pltpu.CompilerParams(
            dimension_semantics=("arbitrary",), vmem_limit_bytes=28 * 1024 * 1024
        ),
        cost_estimate=pl.CostEstimate(
            flops=8 * rows * slots * blk * blk * cols,
            bytes_accessed=10_000_000 + cols * 2_500_000,
            transcendentals=0,
        ),
    )(places, *x_parts, *w_own, *w_other, *earlier)
    return outs[:nz], outs[nz], outs[nz + 1]


OUT_HALVES = ((0, (2, 3)), (1, (1, 3)), (0, (0, 1)), (1, (0, 2)))


def inputs_kernel(nz, spd, counts, groups, unread, places, *refs):
    take = taker(refs)
    chunks = [(take(nz), take(nz), take(1)[0]) for _ in counts]
    take(unread)
    dx_out = [take(len(OUT_HALVES)) for _ in groups]
    dx_all, w_col = take(2)
    step = pl.program_id(0)
    tokens = dx_all.shape[1] // nz
    blk = w_col.shape[-1] // 2
    slots = nz * 2 * spd

    @pl.when(step == 0)
    def _():
        dx_all[...] = jnp.zeros_like(dx_all)

    start = 0
    for count, (w_own, w_other, d_in) in zip(counts, chunks):

        @pl.when((step >= start) & (step < start + count))
        def _(w_own=w_own, w_other=w_other, d_in=d_in):
            for q in range(slots):
                r, i = q // (2 * spd), q % spd
                piece = (w_other if q // spd % 2 else w_own)[r]
                w_col[q * blk : (q + 1) * blk, :blk] = piece[i, 0]
                w_col[q * blk : (q + 1) * blk, blk:] = piece[spd + i, 0]
            for p in range(slots // 2):
                share = lax.dot_general(
                    d_in[0],
                    w_col[2 * p * blk : (2 * p + 2) * blk],
                    (((1,), (1,)), ((), ())),
                    preferred_element_type=F32,
                )
                for h in range(2):
                    m, at = place_of(places, step, 2 * p + h, blk)
                    dx_all[m, :, pl.ds(at, blk)] += share[:, h * blk : (h + 1) * blk]

        start += count

    @pl.when(step == pl.num_programs(0) - 1)
    def _():
        half = tokens // 2
        for group, out in zip(groups, dx_out):
            for ref, (h, ms) in zip(out, OUT_HALVES):
                for i, m in enumerate(ms):
                    for k, r in enumerate(group):
                        rows = dx_all[m, r * tokens + h * half : r * tokens + (h + 1) * half]
                        ref[i, k * half : (k + 1) * half] = rows.astype(BF16)


def inputs_call(places, nw, tokens, features, chunks, groups, earlier):
    nz = len(chunks[0][0])
    parts, _, blk, _ = chunks[0][0][0].shape
    spd = parts // 2
    rows, slots = nz * tokens, nz * 2 * spd
    counts = tuple(c[0][1].shape[1] for c in chunks)
    in_specs, operands, start = [], [], 0
    for count, (w_own, w_other, d) in zip(counts, chunks):

        def at(j, start=start, count=count):
            return jnp.clip(j - start, 0, count - 1)

        block = pl.BlockSpec((2 * spd, 1, blk, blk), lambda j, s, at=at: (0, at(j), 0, 0))
        block0 = pl.BlockSpec(
            (2 * spd, 1, blk, blk), lambda j, s, at=at, start=start: (0, at(j) + start, 0, 0)
        )
        in_specs += ([block0] + [block] * (nz - 1)) * 2
        in_specs += [pl.BlockSpec((1, rows, 2 * blk), lambda j, s, at=at: (at(j), 0, 0))]
        operands += [*w_own, *w_other, d]
        start += count
    in_specs += [ANY] * len(earlier)
    operands += earlier
    shapes = [(2, len(g) * tokens // 2, features) for g in groups for _ in OUT_HALVES]
    outs = pl.pallas_call(
        functools.partial(inputs_kernel, nz, spd, counts, groups, len(earlier)),
        grid_spec=pltpu.PrefetchScalarGridSpec(
            num_scalar_prefetch=1,
            grid=(start,),
            in_specs=in_specs,
            out_specs=[
                pl.BlockSpec(s, lambda j, s_: (0, 0, 0), pipeline_mode=pl.Buffered(1)) for s in shapes
            ],
            scratch_shapes=[
                pltpu.VMEM((nw, rows, features), F32),
                pltpu.VMEM((slots * blk, 2 * blk), BF16),
            ],
        ),
        out_shape=[jax.ShapeDtypeStruct(s, BF16) for s in shapes],
        compiler_params=pltpu.CompilerParams(
            dimension_semantics=("arbitrary",), vmem_limit_bytes=40 * 1024 * 1024
        ),
        cost_estimate=pl.CostEstimate(
            flops=4 * rows * slots * blk * blk * start,
            bytes_accessed=20_000_000,
            transcendentals=0,
        ),
    )(places, *operands)
    n = len(OUT_HALVES)
    return [outs[g * n : (g + 1) * n] for g in range(len(groups))]


def hold(values, *earlier):
    n = len(values)
    return pl.pallas_call(
        lambda *refs: None,
        in_specs=[ANY] * (n + len(earlier)),
        out_specs=[ANY] * n,
        out_shape=[jax.ShapeDtypeStruct(v.shape, v.dtype) for v in values],
        input_output_aliases={i: i for i in range(n)},
    )(*values, *earlier)


VMEM = pl.BlockSpec(memory_space=pltpu.VMEM)
SMEM = pl.BlockSpec(memory_space=pltpu.SMEM)


def message_blocks(nz, cols, spd, blk, bounds, where):
    for k, (r, lo, hi) in enumerate(bounds):
        first = lax.rem(where[0] + r, nz) * cols + lo
        for j in range(hi - lo):
            yield k, j, first + j, pl.ds(pl.multiple_of((first + j) * blk, blk), blk)


def pack_kernel(nz, cols, spd, bounds, where, gate, up, cot, *outs):
    for k, j, col, at in message_blocks(nz, cols, spd, gate.shape[-1], bounds, where):
        for i in range(spd):
            outs[k][i, j] = gate[col, i]
            outs[k][spd + i, j] = up[col, i]
        outs[k][2 * spd, j] = cot[:, at]


def pack_call(nz, bounds, where, gate, up, cot):
    all_cols, spd, blk, _ = gate.shape
    cols = all_cols // nz
    return pl.pallas_call(
        functools.partial(pack_kernel, nz, cols, spd, bounds),
        in_specs=[SMEM] + [VMEM] * 3,
        out_specs=[VMEM] * len(bounds),
        out_shape=[
            jax.ShapeDtypeStruct((2 * spd + 1, hi - lo, blk, blk), BF16) for _, lo, hi in bounds
        ],
        compiler_params=pltpu.CompilerParams(vmem_limit_bytes=20 * 1024 * 1024),
        cost_estimate=pl.CostEstimate(flops=0, bytes_accessed=10_000_000, transcendentals=0),
    )(where, gate, up, cot)


def unpack_kernel(nz, cols, spd, bounds, where, *refs):
    parts = refs[: len(bounds)]
    hidden, gate, up = refs[len(bounds) :]
    for k, j, col, at in message_blocks(nz, cols, spd, gate.shape[-1], bounds, where):
        for i in range(spd):
            gate[col, i] = parts[k][i, j]
            up[col, i] = parts[k][spd + i, j]
        hidden[:, at] = parts[k][2 * spd, j]


def unpack_call(nz, bounds, where, parts, hidden, gate):
    all_cols, spd, blk, _ = gate.shape
    cols = all_cols // nz
    return pl.pallas_call(
        functools.partial(unpack_kernel, nz, cols, spd, bounds),
        in_specs=[SMEM] + [VMEM] * len(bounds),
        out_specs=[VMEM] * 3,
        out_shape=[jax.ShapeDtypeStruct(a.shape, BF16) for a in (hidden, gate, gate)],
        compiler_params=pltpu.CompilerParams(vmem_limit_bytes=20 * 1024 * 1024),
        cost_estimate=pl.CostEstimate(flops=0, bytes_accessed=10_000_000, transcendentals=0),
    )(where, *parts)


def moved_tokens(narrow, nw, inputs, gate_blocks, up_blocks, pattern, grad_hidden):
    nz = narrow // 2
    tokens, features = inputs.shape
    all_cols, spd, blk, _ = gate_blocks.shape
    cols = all_cols // nz
    me = lax.axis_index("narrow")
    z, core = me // 2, me % 2
    wide = lax.axis_index("wide")
    shifts = sorted(range(1, nz), key=lambda r: -min(r, nz - r))

    def along_z(a, s):
        with jax.named_scope(f"along_z{s}"):
            return lax.ppermute(a, "narrow", [(i, (i + 2 * s) % narrow) for i in range(narrow)])

    def swap(a):
        with jax.named_scope("swap"):
            return lax.ppermute(a, "narrow", [(i, i ^ 1) for i in range(narrow)])

    def over_wide(a, m):
        with jax.named_scope(f"wide{m}"):
            return lax.ppermute(a, "wide", [(i, i ^ m) for i in range(nw)])

    where = z.reshape(1).astype(jnp.int32)
    mine = lax.dynamic_slice_in_dim(pattern, cols * z, cols, 0)
    slot_of = jnp.stack(
        [
            ((z - r + nz) % nz * 2 + (core ^ c)) * spd + i
            for r in range(nz)
            for c in range(2)
            for i in range(spd)
        ]
    )
    rows_of = jnp.take(mine, slot_of, axis=1)
    per_device = features // blk
    places = jnp.stack([(rows_of // per_device) ^ wide, rows_of % per_device], axis=-1)

    edges = [cols * k // CHUNKS for k in range(CHUNKS, -1, -1)]
    edges = [cols - e for e in edges]
    chunks = list(zip(edges[:-1], edges[1:]))
    bounds = [(0, 0, cols)] + [(r, lo, hi) for lo, hi in chunks for r in shifts]
    own, *messages = pack_call(nz, bounds, where, gate_blocks, up_blocks, grad_hidden)

    half = tokens // 2
    x_z = {r: along_z(inputs, r) for r in reversed(shifts)}
    x_parts, layout = [], []
    for group in ([0], list(range(1, nz))):
        pieces = [inputs if r == 0 else x_z[r] for r in group]
        a, b = (
            jnp.concatenate([p[h * half : (h + 1) * half] for p in pieces], axis=0)
            for h in range(2)
        )
        if x_parts:
            a, b = hold([a, b], *x_parts[-2:], *messages[:1])
        n = len(group) * half
        ax, by = over_wide(a, 1), over_wide(b, 2)
        far_a = over_wide(jnp.concatenate([a, ax], axis=0), 2)
        far_b = over_wide(jnp.concatenate([b, by], axis=0), 1)
        x_parts += [a, b, ax, by, far_a, far_b]
        for h, ms in ((0, (0,)), (1, (0,)), (0, (1,)), (1, (2,)), (0, (2, 3)), (1, (1, 3))):
            layout.append(
                tuple(
                    (i * n + k * half, m, r * tokens + h * half, half)
                    for i, m in enumerate(ms)
                    for k, r in enumerate(group)
                )
            )

    earlier = [x_z[r] for r in shifts]
    weights, other = [], None
    for lo, hi in chunks:
        now, messages = messages[: nz - 1], messages[nz - 1 :]
        now = [hold([a], e)[0] for a, e in zip(now, earlier)]
        now = earlier = [along_z(a, r) for a, r in zip(now, shifts)]
        if other is None:
            other = swap(*hold([own], *now))
        in_order = [now[shifts.index(r)] for r in range(1, nz)]
        weights.append(([own] + in_order, [other] + [swap(a) for a in in_order]))

    order = [*shifts, 0]
    groups = [order[: (nz + 1) // 2], order[(nz + 1) // 2 :]]
    columns, sent, parts, back, sums = [], [], [], [], []
    for k, ((lo, hi), (w_own, w_other)) in enumerate(zip(chunks, weights)):
        g_own, g_other, d = forward_call(
            lo, nw, tokens, places[lo:hi], tuple(layout), x_parts, w_own, w_other, sums
        )
        columns.append((w_own, w_other, d))
        if k + 1 < len(chunks):
            beside = weights[k + 1][0][1:]
        else:
            dx = inputs_call(places, nw, tokens, features, columns, groups, [])
            beside = [dx[0][0], *(sent[-1] if sent else [])]
        g_other = swap(*hold([g_other], *beside))
        sums = [(g_own[r].astype(F32) + g_other[r].astype(F32)).astype(BF16) for r in [0, *shifts]]
        now = sums[1:]
        if sent:
            now = [hold([a], e)[0] for a, e in zip(now, sent[-1])]
        sent.append([along_z(a, nz - r) for a, r in zip(now, shifts)])
        parts += [sums[0], *sent[-1]]
        back += [(r, lo, hi) for r in [0, *shifts]]
    hidden, grad_gate, grad_up = unpack_call(nz, back, where, parts, grad_hidden, gate_blocks)

    total, earlier = 0, sent[0]
    step = [a for a, r in zip(sent[-1], shifts) if 2 * r != nz]
    for group, (to_y, to_x, keep_a, keep_b) in zip(groups, dx):
        to_y, to_x = hold([to_y, to_x], *earlier)
        to_y, to_x = over_wide(to_y, 2), over_wide(to_x, 1)
        near_a, pass_a = (keep_a[i].astype(F32) + to_y[i].astype(F32) for i in range(2))
        near_b, pass_b = (keep_b[i].astype(F32) + to_x[i].astype(F32) for i in range(2))
        pass_a, pass_b = hold([pass_a.astype(BF16), pass_b.astype(BF16)], *step)
        step = sent[-1]
        earlier = [pass_a, pass_b]
        pass_a, pass_b = over_wide(pass_a, 1), over_wide(pass_b, 2)
        halves = near_a + pass_a.astype(F32), near_b + pass_b.astype(F32)
        shares = []
        for i, r in enumerate(group):
            shares.append(jnp.concatenate([a[i * half : (i + 1) * half] for a in halves], axis=0))
        away = [i for i, r in enumerate(group) if r]
        ready = [shares[i].astype(BF16) for i in away]
        ready = [hold([a], sent[-1][shifts.index(group[i])])[0] for a, i in zip(ready, away)]
        for i, a in zip(away, ready):
            shares[i] = along_z(a, nz - group[i]).astype(F32)
        total = total + sum(shares)
    return hidden, total.astype(BF16), grad_gate, grad_up


def solution(mesh):
    narrow, nw = mesh.shape["narrow"], mesh.shape["wide"]

    def shards(inputs, gate_blocks, up_blocks, pattern, grad_hidden):
        columns = gate_blocks.shape[0]
        if narrow % 2 == 0 and columns % (narrow // 2) == 0 and nw == 4:
            return moved_tokens(
                narrow, nw, inputs, gate_blocks, up_blocks, pattern, grad_hidden
            )
        return gathered_weights(inputs, gate_blocks, up_blocks, pattern, grad_hidden)

    placed = (
        P("narrow", "wide"),
        P("wide", "narrow", None, None),
        P("wide", "narrow", None, None),
        P("wide", None),
        P("narrow", "wide"),
    )
    return jax.shard_map(
        shards,
        mesh=mesh,
        in_specs=placed,
        out_specs=(
            P("narrow", "wide"),
            P("narrow", "wide"),
            P("wide", "narrow", None, None),
            P("wide", "narrow", None, None),
        ),
        check_vma=False,
    )
```

```python
import functools

import jax
import jax.numpy as jnp
from jax import lax
from jax.experimental import pallas as pl
from jax.experimental.pallas import tpu as pltpu
from jax.sharding import PartitionSpec as P


def silu_parts(gate_sum):
    sigmoid_value = jax.nn.sigmoid(gate_sum)
    return (gate_sum * sigmoid_value, sigmoid_value * (1.0 + gate_sum * (1.0 - sigmoid_value)))


def gathered_weights(inputs, gate_blocks, up_blocks, pattern, grad_hidden):
    tokens_here = inputs.shape[0]
    block_size = gate_blocks.shape[2]
    columns = gate_blocks.shape[0]
    full_inputs = lax.all_gather(inputs, "wide", axis=1, tiled=True)
    row_blocks = full_inputs.shape[1] // block_size
    input_blocks = full_inputs.reshape(tokens_here, row_blocks, block_size)
    picked = jnp.take(input_blocks, pattern, axis=1)
    gate_all = lax.all_gather(gate_blocks, "narrow", axis=1, tiled=True)
    up_all = lax.all_gather(up_blocks, "narrow", axis=1, tiled=True)
    gate_sum = jnp.einsum("tjkb,jkbc->tjc", picked, gate_all, preferred_element_type=jnp.float32)
    up_sum = jnp.einsum("tjkb,jkbc->tjc", picked, up_all, preferred_element_type=jnp.float32)
    activation, derivative = silu_parts(gate_sum)
    hidden = (activation * up_sum).astype(jnp.bfloat16)
    cotangent = grad_hidden.reshape(tokens_here, columns, block_size).astype(jnp.float32)
    d_gate = (cotangent * up_sum * derivative).astype(jnp.bfloat16)
    d_up = (cotangent * activation).astype(jnp.bfloat16)
    zero_inputs = jnp.zeros((tokens_here, row_blocks, block_size), jnp.float32)

    def one_slot(k, running):
        gate_slot = lax.dynamic_index_in_dim(gate_all, k, 1, keepdims=False)
        up_slot = lax.dynamic_index_in_dim(up_all, k, 1, keepdims=False)
        contribution = jnp.einsum(
            "tjc,jbc->tjb", d_gate, gate_slot, preferred_element_type=jnp.float32
        )
        contribution = contribution + jnp.einsum(
            "tjc,jbc->tjb", d_up, up_slot, preferred_element_type=jnp.float32
        )
        targets = lax.dynamic_index_in_dim(pattern, k, 1, keepdims=False)
        return running.at[:, targets].add(contribution)

    partial_inputs = lax.fori_loop(0, gate_all.shape[1], one_slot, zero_inputs)
    grad_inputs = lax.psum_scatter(
        partial_inputs.reshape(tokens_here, row_blocks * block_size).astype(jnp.bfloat16),
        "wide",
        scatter_dimension=1,
        tiled=True,
    )
    gate_terms = jnp.einsum("tjkb,tjc->jkbc", picked, d_gate, preferred_element_type=jnp.float32)
    up_terms = jnp.einsum("tjkb,tjc->jkbc", picked, d_up, preferred_element_type=jnp.float32)
    grad_gate = lax.psum_scatter(
        gate_terms.astype(jnp.bfloat16), "narrow", scatter_dimension=1, tiled=True
    )
    grad_up = lax.psum_scatter(
        up_terms.astype(jnp.bfloat16), "narrow", scatter_dimension=1, tiled=True
    )
    return hidden.reshape(tokens_here, columns * block_size), grad_inputs, grad_gate, grad_up


BF16, F32 = jnp.bfloat16, jnp.float32
CHUNKS = 2


ANY = pl.BlockSpec(memory_space=pl.ANY)


def taker(refs):
    refs = list(refs)

    def take(n):
        out = refs[:n]
        del refs[:n]
        return out

    return take


def place_of(places, step, q, blk):
    return places[step, q, 0], pl.multiple_of(places[step, q, 1] * blk, blk)


def forward_kernel(nz, nw, spd, unread, layout, places, *refs):
    take = taker(refs)
    x_in = take(len(layout))
    w_own, w_other = take(nz), take(nz)
    take(unread)
    (g_own, g_other, d_out) = take(nz), take(1)[0], take(1)[0]
    x_all, x_col, w_col, sems = take(4)
    step = pl.program_id(0)
    tokens = d_out.shape[1] // nz
    blk = d_out.shape[-1] // 2
    slots = nz * 2 * spd

    @pl.when(step == 0)
    def _():
        copies = []
        for source, pieces in zip(x_in, layout):
            for at, m, rows, n in pieces:
                target = x_all.at[m, pl.ds(rows, n)]
                sem = sems.at[len(copies)]
                copies.append(pltpu.make_async_copy(source.at[pl.ds(at, n)], target, sem))
        for c in copies:
            c.start()
        for c in copies:
            c.wait()

    for q in range(slots):
        r, i = q // (2 * spd), q % spd
        piece = (w_other if q // spd % 2 else w_own)[r]
        m, at = place_of(places, step, q, blk)
        x_col[:, q * blk : (q + 1) * blk] = x_all[m, :, pl.ds(at, blk)]
        w_col[q * blk : (q + 1) * blk, :blk] = piece[i, 0]
        w_col[q * blk : (q + 1) * blk, blk:] = piece[spd + i, 0]
    both = jnp.dot(x_col[...], w_col[...], preferred_element_type=F32)
    gate, up = both[:, :blk], both[:, blk:]
    activation, derivative = silu_parts(gate)
    hidden = (activation * up).astype(BF16)
    cotangent = jnp.concatenate([w[2 * spd, 0] for w in w_own], axis=0).astype(F32)
    d_out[0, :, :blk] = (cotangent * up * derivative).astype(BF16)
    d_out[0, :, blk:] = (cotangent * activation).astype(BF16)
    for r in range(nz):
        g_own[r][2 * spd, 0] = hidden[r * tokens : (r + 1) * tokens]
        g_other[r, 2 * spd, 0] = jnp.zeros((tokens, blk), BF16)
    for p in range(slots // 2):
        grads = lax.dot_general(
            x_col[:, 2 * p * blk : (2 * p + 2) * blk],
            d_out[0],
            (((0,), (0,)), ((), ())),
            preferred_element_type=F32,
        ).astype(BF16)
        for h in range(2):
            q = 2 * p + h
            r, i = q // (2 * spd), q % spd
            rows = grads[h * blk : (h + 1) * blk]
            target = g_other.at[r] if q // spd % 2 else g_own[r]
            target[i, 0] = rows[:, :blk]
            target[spd + i, 0] = rows[:, blk:]


def forward_call(lo, nw, tokens, places, layout, x_parts, w_own, w_other, earlier):
    nz, features = len(w_own), x_parts[0].shape[1]
    parts, cols, blk, _ = w_own[1].shape
    spd = parts // 2
    rows, slots = nz * tokens, nz * 2 * spd
    own = pl.BlockSpec((parts, 1, blk, blk), lambda j, s: (0, j, 0, 0))
    own0 = pl.BlockSpec((parts, 1, blk, blk), lambda j, s: (0, j + lo, 0, 0))
    other = pl.BlockSpec((2 * spd, 1, blk, blk), lambda j, s: (0, j, 0, 0))
    other0 = pl.BlockSpec((2 * spd, 1, blk, blk), lambda j, s: (0, j + lo, 0, 0))
    every = pl.BlockSpec((nz, parts, 1, blk, blk), lambda j, s: (0, 0, j, 0, 0))
    d_spec = pl.BlockSpec((1, rows, 2 * blk), lambda j, s: (j, 0, 0))
    outs = pl.pallas_call(
        functools.partial(forward_kernel, nz, nw, spd, len(earlier), layout),
        grid_spec=pltpu.PrefetchScalarGridSpec(
            num_scalar_prefetch=1,
            grid=(cols,),
            in_specs=[ANY] * len(x_parts)
            + [own0]
            + [own] * (nz - 1)
            + [other0]
            + [other] * (nz - 1)
            + [ANY] * len(earlier),
            out_specs=[own] * nz + [every, d_spec],
            scratch_shapes=[
                pltpu.VMEM((nw, rows, features), BF16),
                pltpu.VMEM((rows, slots * blk), BF16),
                pltpu.VMEM((slots * blk, 2 * blk), BF16),
                pltpu.SemaphoreType.DMA((sum(len(p) for p in layout),)),
            ],
        ),
        out_shape=[jax.ShapeDtypeStruct(w_own[1].shape, BF16)] * nz
        + [
            jax.ShapeDtypeStruct((nz, *w_own[1].shape), BF16),
            jax.ShapeDtypeStruct((cols, rows, 2 * blk), BF16),
        ],
        compiler_params=pltpu.CompilerParams(
            dimension_semantics=("arbitrary",), vmem_limit_bytes=28 * 1024 * 1024
        ),
        cost_estimate=pl.CostEstimate(
            flops=8 * rows * slots * blk * blk * cols,
            bytes_accessed=10_000_000 + cols * 2_500_000,
            transcendentals=0,
        ),
    )(places, *x_parts, *w_own, *w_other, *earlier)
    return outs[:nz], outs[nz], outs[nz + 1]


OUT_HALVES = ((0, (2, 3)), (1, (1, 3)), (0, (0, 1)), (1, (0, 2)))


def inputs_kernel(nz, spd, counts, groups, unread, places, *refs):
    take = taker(refs)
    chunks = [(take(nz), take(nz), take(1)[0]) for _ in counts]
    take(unread)
    dx_out = [take(len(OUT_HALVES)) for _ in groups]
    dx_all, w_col = take(2)
    step = pl.program_id(0)
    tokens = dx_all.shape[1] // nz
    blk = w_col.shape[-1] // 2
    slots = nz * 2 * spd

    @pl.when(step == 0)
    def _():
        dx_all[...] = jnp.zeros_like(dx_all)

    start = 0
    for count, (w_own, w_other, d_in) in zip(counts, chunks):

        @pl.when((step >= start) & (step < start + count))
        def _(w_own=w_own, w_other=w_other, d_in=d_in):
            for q in range(slots):
                r, i = q // (2 * spd), q % spd
                piece = (w_other if q // spd % 2 else w_own)[r]
                w_col[q * blk : (q + 1) * blk, :blk] = piece[i, 0]
                w_col[q * blk : (q + 1) * blk, blk:] = piece[spd + i, 0]
            for p in range(slots // 2):
                share = lax.dot_general(
                    d_in[0],
                    w_col[2 * p * blk : (2 * p + 2) * blk],
                    (((1,), (1,)), ((), ())),
                    preferred_element_type=F32,
                )
                for h in range(2):
                    m, at = place_of(places, step, 2 * p + h, blk)
                    dx_all[m, :, pl.ds(at, blk)] += share[:, h * blk : (h + 1) * blk]

        start += count

    @pl.when(step == pl.num_programs(0) - 1)
    def _():
        half = tokens // 2
        for group, out in zip(groups, dx_out):
            for ref, (h, ms) in zip(out, OUT_HALVES):
                for i, m in enumerate(ms):
                    for k, r in enumerate(group):
                        rows = dx_all[m, r * tokens + h * half : r * tokens + (h + 1) * half]
                        ref[i, k * half : (k + 1) * half] = rows.astype(BF16)


def inputs_call(places, nw, tokens, features, chunks, groups, earlier):
    nz = len(chunks[0][0])
    parts, _, blk, _ = chunks[0][0][0].shape
    spd = parts // 2
    rows, slots = nz * tokens, nz * 2 * spd
    counts = tuple(c[0][1].shape[1] for c in chunks)
    in_specs, operands, start = [], [], 0
    for count, (w_own, w_other, d) in zip(counts, chunks):

        def at(j, start=start, count=count):
            return jnp.clip(j - start, 0, count - 1)

        block = pl.BlockSpec((2 * spd, 1, blk, blk), lambda j, s, at=at: (0, at(j), 0, 0))
        block0 = pl.BlockSpec(
            (2 * spd, 1, blk, blk), lambda j, s, at=at, start=start: (0, at(j) + start, 0, 0)
        )
        in_specs += ([block0] + [block] * (nz - 1)) * 2
        in_specs += [pl.BlockSpec((1, rows, 2 * blk), lambda j, s, at=at: (at(j), 0, 0))]
        operands += [*w_own, *w_other, d]
        start += count
    in_specs += [ANY] * len(earlier)
    operands += earlier
    shapes = [(2, len(g) * tokens // 2, features) for g in groups for _ in OUT_HALVES]
    outs = pl.pallas_call(
        functools.partial(inputs_kernel, nz, spd, counts, groups, len(earlier)),
        grid_spec=pltpu.PrefetchScalarGridSpec(
            num_scalar_prefetch=1,
            grid=(start,),
            in_specs=in_specs,
            out_specs=[
                pl.BlockSpec(s, lambda j, s_: (0, 0, 0), pipeline_mode=pl.Buffered(1)) for s in shapes
            ],
            scratch_shapes=[
                pltpu.VMEM((nw, rows, features), F32),
                pltpu.VMEM((slots * blk, 2 * blk), BF16),
            ],
        ),
        out_shape=[jax.ShapeDtypeStruct(s, BF16) for s in shapes],
        compiler_params=pltpu.CompilerParams(
            dimension_semantics=("arbitrary",), vmem_limit_bytes=40 * 1024 * 1024
        ),
        cost_estimate=pl.CostEstimate(
            flops=4 * rows * slots * blk * blk * start,
            bytes_accessed=20_000_000,
            transcendentals=0,
        ),
    )(places, *operands)
    n = len(OUT_HALVES)
    return [outs[g * n : (g + 1) * n] for g in range(len(groups))]


def hold(values, *earlier):
    n = len(values)
    return pl.pallas_call(
        lambda *refs: None,
        in_specs=[ANY] * (n + len(earlier)),
        out_specs=[ANY] * n,
        out_shape=[jax.ShapeDtypeStruct(v.shape, v.dtype) for v in values],
        input_output_aliases={i: i for i in range(n)},
    )(*values, *earlier)


VMEM = pl.BlockSpec(memory_space=pltpu.VMEM)
SMEM = pl.BlockSpec(memory_space=pltpu.SMEM)


def message_blocks(nz, cols, spd, blk, bounds, where):
    for k, (r, lo, hi) in enumerate(bounds):
        first = lax.rem(where[0] + r, nz) * cols + lo
        for j in range(hi - lo):
            yield k, j, first + j, pl.ds(pl.multiple_of((first + j) * blk, blk), blk)


def pack_kernel(nz, cols, spd, bounds, where, gate, up, cot, *outs):
    for k, j, col, at in message_blocks(nz, cols, spd, gate.shape[-1], bounds, where):
        for i in range(spd):
            outs[k][i, j] = gate[col, i]
            outs[k][spd + i, j] = up[col, i]
        outs[k][2 * spd, j] = cot[:, at]


def pack_call(nz, bounds, where, gate, up, cot):
    all_cols, spd, blk, _ = gate.shape
    cols = all_cols // nz
    return pl.pallas_call(
        functools.partial(pack_kernel, nz, cols, spd, bounds),
        in_specs=[SMEM] + [VMEM] * 3,
        out_specs=[VMEM] * len(bounds),
        out_shape=[
            jax.ShapeDtypeStruct((2 * spd + 1, hi - lo, blk, blk), BF16) for _, lo, hi in bounds
        ],
        compiler_params=pltpu.CompilerParams(vmem_limit_bytes=20 * 1024 * 1024),
        cost_estimate=pl.CostEstimate(flops=0, bytes_accessed=10_000_000, transcendentals=0),
    )(where, gate, up, cot)


def unpack_kernel(nz, cols, spd, bounds, where, *refs):
    parts = refs[: len(bounds)]
    hidden, gate, up = refs[len(bounds) :]
    for k, j, col, at in message_blocks(nz, cols, spd, gate.shape[-1], bounds, where):
        for i in range(spd):
            gate[col, i] = parts[k][i, j]
            up[col, i] = parts[k][spd + i, j]
        hidden[:, at] = parts[k][2 * spd, j]


def unpack_call(nz, bounds, where, parts, hidden, gate):
    all_cols, spd, blk, _ = gate.shape
    cols = all_cols // nz
    return pl.pallas_call(
        functools.partial(unpack_kernel, nz, cols, spd, bounds),
        in_specs=[SMEM] + [VMEM] * len(bounds),
        out_specs=[VMEM] * 3,
        out_shape=[jax.ShapeDtypeStruct(a.shape, BF16) for a in (hidden, gate, gate)],
        compiler_params=pltpu.CompilerParams(vmem_limit_bytes=20 * 1024 * 1024),
        cost_estimate=pl.CostEstimate(flops=0, bytes_accessed=10_000_000, transcendentals=0),
    )(where, *parts)


def moved_tokens(narrow, nw, inputs, gate_blocks, up_blocks, pattern, grad_hidden):
    nz = narrow // 2
    tokens, features = inputs.shape
    all_cols, spd, blk, _ = gate_blocks.shape
    cols = all_cols // nz
    me = lax.axis_index("narrow")
    z, core = me // 2, me % 2
    wide = lax.axis_index("wide")
    shifts = sorted(range(1, nz), key=lambda r: -min(r, nz - r))

    def along_z(a, s):
        with jax.named_scope(f"along_z{s}"):
            return lax.ppermute(a, "narrow", [(i, (i + 2 * s) % narrow) for i in range(narrow)])

    def swap(a):
        with jax.named_scope("swap"):
            return lax.ppermute(a, "narrow", [(i, i ^ 1) for i in range(narrow)])

    def over_wide(a, m):
        with jax.named_scope(f"wide{m}"):
            return lax.ppermute(a, "wide", [(i, i ^ m) for i in range(nw)])

    where = z.reshape(1).astype(jnp.int32)
    mine = lax.dynamic_slice_in_dim(pattern, cols * z, cols, 0)
    slot_of = jnp.stack(
        [
            ((z - r + nz) % nz * 2 + (core ^ c)) * spd + i
            for r in range(nz)
            for c in range(2)
            for i in range(spd)
        ]
    )
    rows_of = jnp.take(mine, slot_of, axis=1)
    per_device = features // blk
    places = jnp.stack([(rows_of // per_device) ^ wide, rows_of % per_device], axis=-1)

    edges = [cols * k // CHUNKS for k in range(CHUNKS, -1, -1)]
    edges = [cols - e for e in edges]
    chunks = list(zip(edges[:-1], edges[1:]))
    bounds = [(0, 0, cols)] + [(r, lo, hi) for lo, hi in chunks for r in shifts]
    own, *messages = pack_call(nz, bounds, where, gate_blocks, up_blocks, grad_hidden)

    half = tokens // 2
    x_z = {1: along_z(inputs, 1), 3: along_z(inputs, 3)}
    x_z[2] = along_z(x_z[1], 1)
    x_parts, layout = [], []
    for group in ([0], list(range(1, nz))):
        pieces = [inputs if r == 0 else x_z[r] for r in group]
        a, b = (
            jnp.concatenate([p[h * half : (h + 1) * half] for p in pieces], axis=0)
            for h in range(2)
        )
        if x_parts:
            a, b = hold([a, b], *x_parts[-2:], *messages[:1])
        n = len(group) * half
        ax, by = over_wide(a, 1), over_wide(b, 2)
        far_a = over_wide(jnp.concatenate([a, ax], axis=0), 2)
        far_b = over_wide(jnp.concatenate([b, by], axis=0), 1)
        x_parts += [a, b, ax, by, far_a, far_b]
        for h, ms in ((0, (0,)), (1, (0,)), (0, (1,)), (1, (2,)), (0, (2, 3)), (1, (1, 3))):
            layout.append(
                tuple(
                    (i * n + k * half, m, r * tokens + h * half, half)
                    for i, m in enumerate(ms)
                    for k, r in enumerate(group)
                )
            )

    earlier = [x_z[2] for r in shifts]
    weights, other = [], None
    for lo, hi in chunks:
        now, messages = messages[: nz - 1], messages[nz - 1 :]
        now = [hold([a], e)[0] for a, e in zip(now, earlier)]
        now = earlier = [along_z(a, r) for a, r in zip(now, shifts)]
        if other is None:
            other = swap(*hold([own], *now))
        in_order = [now[shifts.index(r)] for r in range(1, nz)]
        weights.append(([own] + in_order, [other] + [swap(a) for a in in_order]))

    order = [*shifts, 0]
    groups = [order[: (nz + 1) // 2], order[(nz + 1) // 2 :]]
    columns, sent, parts, back, sums = [], [], [], [], []
    for k, ((lo, hi), (w_own, w_other)) in enumerate(zip(chunks, weights)):
        g_own, g_other, d = forward_call(
            lo, nw, tokens, places[lo:hi], tuple(layout), x_parts, w_own, w_other, sums
        )
        columns.append((w_own, w_other, d))
        if k + 1 < len(chunks):
            beside = weights[k + 1][0][1:]
        else:
            dx = inputs_call(places, nw, tokens, features, columns, groups, [])
            beside = [dx[0][0], *(sent[-1] if sent else [])]
        g_other = swap(*hold([g_other], *beside))
        sums = [(g_own[r].astype(F32) + g_other[r].astype(F32)).astype(BF16) for r in [0, *shifts]]
        now = sums[1:]
        if sent:
            now = [hold([a], e)[0] for a, e in zip(now, sent[-1])]
        sent.append([along_z(a, nz - r) for a, r in zip(now, shifts)])
        parts += [sums[0], *sent[-1]]
        back += [(r, lo, hi) for r in [0, *shifts]]
    hidden, grad_gate, grad_up = unpack_call(nz, back, where, parts, grad_hidden, gate_blocks)

    total, moved, earlier = None, [], sent[0]
    step = [a for a, r in zip(sent[-1], shifts) if 2 * r != nz]
    for group, (to_y, to_x, keep_a, keep_b) in zip(groups, dx):
        to_y, to_x = hold([to_y, to_x], *earlier)
        to_y, to_x = over_wide(to_y, 2), over_wide(to_x, 1)
        near_a, pass_a = (keep_a[i].astype(F32) + to_y[i].astype(F32) for i in range(2))
        near_b, pass_b = (keep_b[i].astype(F32) + to_x[i].astype(F32) for i in range(2))
        pass_a, pass_b = hold([pass_a.astype(BF16), pass_b.astype(BF16)], *step)
        earlier = [pass_a, pass_b]
        pass_a, pass_b = over_wide(pass_a, 1), over_wide(pass_b, 2)
        halves = near_a + pass_a.astype(F32), near_b + pass_b.astype(F32)
        shares = []
        for i, r in enumerate(group):
            shares.append(jnp.concatenate([a[i * half : (i + 1) * half] for a in halves], axis=0))
        if not moved:
            moved = [along_z(*hold([shares[0].astype(BF16)], *sent[-1]), nz - 1)]
            shares = [shares[1] + moved[0].astype(F32)]
            step = moved
        arrived = along_z(shares[0].astype(BF16), nz - (3 if total is not None else 1))
        total = arrived.astype(F32) if total is None else total + arrived.astype(F32) + shares[1]
    return hidden, total.astype(BF16), grad_gate, grad_up


def solution(mesh):
    narrow, nw = mesh.shape["narrow"], mesh.shape["wide"]

    def shards(inputs, gate_blocks, up_blocks, pattern, grad_hidden):
        columns = gate_blocks.shape[0]
        if narrow % 2 == 0 and columns % (narrow // 2) == 0 and narrow == 8 and nw == 4:
            return moved_tokens(
                narrow, nw, inputs, gate_blocks, up_blocks, pattern, grad_hidden
            )
        return gathered_weights(inputs, gate_blocks, up_blocks, pattern, grad_hidden)

    placed = (
        P("narrow", "wide"),
        P("wide", "narrow", None, None),
        P("wide", "narrow", None, None),
        P("wide", None),
        P("narrow", "wide"),
    )
    return jax.shard_map(
        shards,
        mesh=mesh,
        in_specs=placed,
        out_specs=(
            P("narrow", "wide"),
            P("narrow", "wide"),
            P("wide", "narrow", None, None),
            P("wide", "narrow", None, None),
        ),
        check_vma=False,
    )
```

```python
import functools

import jax
import jax.numpy as jnp
from jax import lax
from jax.experimental import pallas as pl
from jax.experimental.pallas import tpu as pltpu
from jax.sharding import PartitionSpec as P


def silu_parts(gate_sum):
    sigmoid_value = jax.nn.sigmoid(gate_sum)
    return (gate_sum * sigmoid_value, sigmoid_value * (1.0 + gate_sum * (1.0 - sigmoid_value)))


def gathered_weights(inputs, gate_blocks, up_blocks, pattern, grad_hidden):
    tokens_here = inputs.shape[0]
    block_size = gate_blocks.shape[2]
    columns = gate_blocks.shape[0]
    full_inputs = lax.all_gather(inputs, "wide", axis=1, tiled=True)
    row_blocks = full_inputs.shape[1] // block_size
    input_blocks = full_inputs.reshape(tokens_here, row_blocks, block_size)
    picked = jnp.take(input_blocks, pattern, axis=1)
    gate_all = lax.all_gather(gate_blocks, "narrow", axis=1, tiled=True)
    up_all = lax.all_gather(up_blocks, "narrow", axis=1, tiled=True)
    gate_sum = jnp.einsum("tjkb,jkbc->tjc", picked, gate_all, preferred_element_type=jnp.float32)
    up_sum = jnp.einsum("tjkb,jkbc->tjc", picked, up_all, preferred_element_type=jnp.float32)
    activation, derivative = silu_parts(gate_sum)
    hidden = (activation * up_sum).astype(jnp.bfloat16)
    cotangent = grad_hidden.reshape(tokens_here, columns, block_size).astype(jnp.float32)
    d_gate = (cotangent * up_sum * derivative).astype(jnp.bfloat16)
    d_up = (cotangent * activation).astype(jnp.bfloat16)
    zero_inputs = jnp.zeros((tokens_here, row_blocks, block_size), jnp.float32)

    def one_slot(k, running):
        gate_slot = lax.dynamic_index_in_dim(gate_all, k, 1, keepdims=False)
        up_slot = lax.dynamic_index_in_dim(up_all, k, 1, keepdims=False)
        contribution = jnp.einsum(
            "tjc,jbc->tjb", d_gate, gate_slot, preferred_element_type=jnp.float32
        )
        contribution = contribution + jnp.einsum(
            "tjc,jbc->tjb", d_up, up_slot, preferred_element_type=jnp.float32
        )
        targets = lax.dynamic_index_in_dim(pattern, k, 1, keepdims=False)
        return running.at[:, targets].add(contribution)

    partial_inputs = lax.fori_loop(0, gate_all.shape[1], one_slot, zero_inputs)
    grad_inputs = lax.psum_scatter(
        partial_inputs.reshape(tokens_here, row_blocks * block_size).astype(jnp.bfloat16),
        "wide",
        scatter_dimension=1,
        tiled=True,
    )
    gate_terms = jnp.einsum("tjkb,tjc->jkbc", picked, d_gate, preferred_element_type=jnp.float32)
    up_terms = jnp.einsum("tjkb,tjc->jkbc", picked, d_up, preferred_element_type=jnp.float32)
    grad_gate = lax.psum_scatter(
        gate_terms.astype(jnp.bfloat16), "narrow", scatter_dimension=1, tiled=True
    )
    grad_up = lax.psum_scatter(
        up_terms.astype(jnp.bfloat16), "narrow", scatter_dimension=1, tiled=True
    )
    return hidden.reshape(tokens_here, columns * block_size), grad_inputs, grad_gate, grad_up


BF16, F32 = jnp.bfloat16, jnp.float32
CHUNKS = 2


ANY = pl.BlockSpec(memory_space=pl.ANY)


def taker(refs):
    refs = list(refs)

    def take(n):
        out = refs[:n]
        del refs[:n]
        return out

    return take


def place_of(places, step, q, blk):
    return places[step, q, 0], pl.multiple_of(places[step, q, 1] * blk, blk)


def forward_kernel(nz, nw, spd, unread, layout, places, *refs):
    take = taker(refs)
    x_in = take(len(layout))
    w_own, w_other = take(nz), take(nz)
    take(unread)
    (g_own, g_other, d_out) = take(nz), take(1)[0], take(1)[0]
    x_all, x_col, w_col, sems = take(4)
    step = pl.program_id(0)
    tokens = d_out.shape[1] // nz
    blk = d_out.shape[-1] // 2
    slots = nz * 2 * spd

    @pl.when(step == 0)
    def _():
        copies = []
        for source, pieces in zip(x_in, layout):
            for at, m, rows, n in pieces:
                target = x_all.at[m, pl.ds(rows, n)]
                sem = sems.at[len(copies)]
                copies.append(pltpu.make_async_copy(source.at[pl.ds(at, n)], target, sem))
        for c in copies:
            c.start()
        for c in copies:
            c.wait()

    for q in range(slots):
        r, i = q // (2 * spd), q % spd
        piece = (w_other if q // spd % 2 else w_own)[r]
        m, at = place_of(places, step, q, blk)
        x_col[:, q * blk : (q + 1) * blk] = x_all[m, :, pl.ds(at, blk)]
        w_col[q * blk : (q + 1) * blk, :blk] = piece[i, 0]
        w_col[q * blk : (q + 1) * blk, blk:] = piece[spd + i, 0]
    both = jnp.dot(x_col[...], w_col[...], preferred_element_type=F32)
    gate, up = both[:, :blk], both[:, blk:]
    activation, derivative = silu_parts(gate)
    hidden = (activation * up).astype(BF16)
    cotangent = jnp.concatenate([w[2 * spd, 0] for w in w_own], axis=0).astype(F32)
    d_out[0, :, :blk] = (cotangent * up * derivative).astype(BF16)
    d_out[0, :, blk:] = (cotangent * activation).astype(BF16)
    for r in range(nz):
        g_own[r][2 * spd, 0] = hidden[r * tokens : (r + 1) * tokens]
        g_other[r, 2 * spd, 0] = jnp.zeros((tokens, blk), BF16)
    for p in range(slots // 2):
        grads = lax.dot_general(
            x_col[:, 2 * p * blk : (2 * p + 2) * blk],
            d_out[0],
            (((0,), (0,)), ((), ())),
            preferred_element_type=F32,
        ).astype(BF16)
        for h in range(2):
            q = 2 * p + h
            r, i = q // (2 * spd), q % spd
            rows = grads[h * blk : (h + 1) * blk]
            target = g_other.at[r] if q // spd % 2 else g_own[r]
            target[i, 0] = rows[:, :blk]
            target[spd + i, 0] = rows[:, blk:]


def forward_call(lo, nw, tokens, places, layout, x_parts, w_own, w_other, earlier):
    nz, features = len(w_own), x_parts[0].shape[1]
    parts, cols, blk, _ = w_own[1].shape
    spd = parts // 2
    rows, slots = nz * tokens, nz * 2 * spd
    own = pl.BlockSpec((parts, 1, blk, blk), lambda j, s: (0, j, 0, 0))
    own0 = pl.BlockSpec((parts, 1, blk, blk), lambda j, s: (0, j + lo, 0, 0))
    other = pl.BlockSpec((2 * spd, 1, blk, blk), lambda j, s: (0, j, 0, 0))
    other0 = pl.BlockSpec((2 * spd, 1, blk, blk), lambda j, s: (0, j + lo, 0, 0))
    every = pl.BlockSpec((nz, parts, 1, blk, blk), lambda j, s: (0, 0, j, 0, 0))
    d_spec = pl.BlockSpec((1, rows, 2 * blk), lambda j, s: (j, 0, 0))
    outs = pl.pallas_call(
        functools.partial(forward_kernel, nz, nw, spd, len(earlier), layout),
        grid_spec=pltpu.PrefetchScalarGridSpec(
            num_scalar_prefetch=1,
            grid=(cols,),
            in_specs=[ANY] * len(x_parts)
            + [own0]
            + [own] * (nz - 1)
            + [other0]
            + [other] * (nz - 1)
            + [ANY] * len(earlier),
            out_specs=[own] * nz + [every, d_spec],
            scratch_shapes=[
                pltpu.VMEM((nw, rows, features), BF16),
                pltpu.VMEM((rows, slots * blk), BF16),
                pltpu.VMEM((slots * blk, 2 * blk), BF16),
                pltpu.SemaphoreType.DMA((sum(len(p) for p in layout),)),
            ],
        ),
        out_shape=[jax.ShapeDtypeStruct(w_own[1].shape, BF16)] * nz
        + [
            jax.ShapeDtypeStruct((nz, *w_own[1].shape), BF16),
            jax.ShapeDtypeStruct((cols, rows, 2 * blk), BF16),
        ],
        compiler_params=pltpu.CompilerParams(
            dimension_semantics=("arbitrary",), vmem_limit_bytes=28 * 1024 * 1024
        ),
        cost_estimate=pl.CostEstimate(
            flops=8 * rows * slots * blk * blk * cols,
            bytes_accessed=10_000_000 + cols * 2_500_000,
            transcendentals=0,
        ),
    )(places, *x_parts, *w_own, *w_other, *earlier)
    return outs[:nz], outs[nz], outs[nz + 1]


OUT_HALVES = ((0, (2, 3)), (1, (1, 3)), (0, (0, 1)), (1, (0, 2)))


def inputs_kernel(nz, spd, counts, groups, unread, places, *refs):
    take = taker(refs)
    chunks = [(take(nz), take(nz), take(1)[0]) for _ in counts]
    take(unread)
    dx_out = [take(len(OUT_HALVES)) for _ in groups]
    dx_all, w_col = take(2)
    step = pl.program_id(0)
    tokens = dx_all.shape[1] // nz
    blk = w_col.shape[-1] // 2
    slots = nz * 2 * spd

    @pl.when(step == 0)
    def _():
        dx_all[...] = jnp.zeros_like(dx_all)

    start = 0
    for count, (w_own, w_other, d_in) in zip(counts, chunks):

        @pl.when((step >= start) & (step < start + count))
        def _(w_own=w_own, w_other=w_other, d_in=d_in):
            for q in range(slots):
                r, i = q // (2 * spd), q % spd
                piece = (w_other if q // spd % 2 else w_own)[r]
                w_col[q * blk : (q + 1) * blk, :blk] = piece[i, 0]
                w_col[q * blk : (q + 1) * blk, blk:] = piece[spd + i, 0]
            for p in range(slots // 2):
                share = lax.dot_general(
                    d_in[0],
                    w_col[2 * p * blk : (2 * p + 2) * blk],
                    (((1,), (1,)), ((), ())),
                    preferred_element_type=F32,
                )
                for h in range(2):
                    m, at = place_of(places, step, 2 * p + h, blk)
                    dx_all[m, :, pl.ds(at, blk)] += share[:, h * blk : (h + 1) * blk]

        start += count

    @pl.when(step == pl.num_programs(0) - 1)
    def _():
        half = tokens // 2
        for group, out in zip(groups, dx_out):
            for ref, (h, ms) in zip(out, OUT_HALVES):
                for i, m in enumerate(ms):
                    for k, r in enumerate(group):
                        rows = dx_all[m, r * tokens + h * half : r * tokens + (h + 1) * half]
                        ref[i, k * half : (k + 1) * half] = rows.astype(BF16)


def inputs_call(places, nw, tokens, features, chunks, groups, earlier):
    nz = len(chunks[0][0])
    parts, _, blk, _ = chunks[0][0][0].shape
    spd = parts // 2
    rows, slots = nz * tokens, nz * 2 * spd
    counts = tuple(c[0][1].shape[1] for c in chunks)
    in_specs, operands, start = [], [], 0
    for count, (w_own, w_other, d) in zip(counts, chunks):

        def at(j, start=start, count=count):
            return jnp.clip(j - start, 0, count - 1)

        block = pl.BlockSpec((2 * spd, 1, blk, blk), lambda j, s, at=at: (0, at(j), 0, 0))
        block0 = pl.BlockSpec(
            (2 * spd, 1, blk, blk), lambda j, s, at=at, start=start: (0, at(j) + start, 0, 0)
        )
        in_specs += ([block0] + [block] * (nz - 1)) * 2
        in_specs += [pl.BlockSpec((1, rows, 2 * blk), lambda j, s, at=at: (at(j), 0, 0))]
        operands += [*w_own, *w_other, d]
        start += count
    in_specs += [ANY] * len(earlier)
    operands += earlier
    shapes = [(2, len(g) * tokens // 2, features) for g in groups for _ in OUT_HALVES]
    outs = pl.pallas_call(
        functools.partial(inputs_kernel, nz, spd, counts, groups, len(earlier)),
        grid_spec=pltpu.PrefetchScalarGridSpec(
            num_scalar_prefetch=1,
            grid=(start,),
            in_specs=in_specs,
            out_specs=[
                pl.BlockSpec(s, lambda j, s_: (0, 0, 0), pipeline_mode=pl.Buffered(1)) for s in shapes
            ],
            scratch_shapes=[
                pltpu.VMEM((nw, rows, features), F32),
                pltpu.VMEM((slots * blk, 2 * blk), BF16),
            ],
        ),
        out_shape=[jax.ShapeDtypeStruct(s, BF16) for s in shapes],
        compiler_params=pltpu.CompilerParams(
            dimension_semantics=("arbitrary",), vmem_limit_bytes=40 * 1024 * 1024
        ),
        cost_estimate=pl.CostEstimate(
            flops=4 * rows * slots * blk * blk * start,
            bytes_accessed=20_000_000,
            transcendentals=0,
        ),
    )(places, *operands)
    n = len(OUT_HALVES)
    return [outs[g * n : (g + 1) * n] for g in range(len(groups))]


def hold(values, *earlier):
    n = len(values)
    return pl.pallas_call(
        lambda *refs: None,
        in_specs=[ANY] * (n + len(earlier)),
        out_specs=[ANY] * n,
        out_shape=[jax.ShapeDtypeStruct(v.shape, v.dtype) for v in values],
        input_output_aliases={i: i for i in range(n)},
    )(*values, *earlier)


VMEM = pl.BlockSpec(memory_space=pltpu.VMEM)
SMEM = pl.BlockSpec(memory_space=pltpu.SMEM)


def message_blocks(nz, cols, spd, blk, bounds, where):
    for k, (r, lo, hi) in enumerate(bounds):
        first = lax.rem(where[0] + r, nz) * cols + lo
        for j in range(hi - lo):
            yield k, j, first + j, pl.ds(pl.multiple_of((first + j) * blk, blk), blk)


def pack_kernel(nz, cols, spd, bounds, where, gate, up, cot, *outs):
    for k, j, col, at in message_blocks(nz, cols, spd, gate.shape[-1], bounds, where):
        for i in range(spd):
            outs[k][i, j] = gate[col, i]
            outs[k][spd + i, j] = up[col, i]
        outs[k][2 * spd, j] = cot[:, at]


def pack_call(nz, bounds, where, gate, up, cot):
    all_cols, spd, blk, _ = gate.shape
    cols = all_cols // nz
    return pl.pallas_call(
        functools.partial(pack_kernel, nz, cols, spd, bounds),
        in_specs=[SMEM] + [VMEM] * 3,
        out_specs=[VMEM] * len(bounds),
        out_shape=[
            jax.ShapeDtypeStruct((2 * spd + 1, hi - lo, blk, blk), BF16) for _, lo, hi in bounds
        ],
        compiler_params=pltpu.CompilerParams(vmem_limit_bytes=20 * 1024 * 1024),
        cost_estimate=pl.CostEstimate(flops=0, bytes_accessed=10_000_000, transcendentals=0),
    )(where, gate, up, cot)


def unpack_kernel(nz, cols, spd, bounds, where, *refs):
    parts = refs[: len(bounds)]
    hidden, gate, up = refs[len(bounds) :]
    for k, j, col, at in message_blocks(nz, cols, spd, gate.shape[-1], bounds, where):
        for i in range(spd):
            gate[col, i] = parts[k][i, j]
            up[col, i] = parts[k][spd + i, j]
        hidden[:, at] = parts[k][2 * spd, j]


def unpack_call(nz, bounds, where, parts, hidden, gate):
    all_cols, spd, blk, _ = gate.shape
    cols = all_cols // nz
    return pl.pallas_call(
        functools.partial(unpack_kernel, nz, cols, spd, bounds),
        in_specs=[SMEM] + [VMEM] * len(bounds),
        out_specs=[VMEM] * 3,
        out_shape=[jax.ShapeDtypeStruct(a.shape, BF16) for a in (hidden, gate, gate)],
        compiler_params=pltpu.CompilerParams(vmem_limit_bytes=20 * 1024 * 1024),
        cost_estimate=pl.CostEstimate(flops=0, bytes_accessed=10_000_000, transcendentals=0),
    )(where, *parts)


def moved_tokens(narrow, nw, inputs, gate_blocks, up_blocks, pattern, grad_hidden):
    nz = narrow // 2
    tokens, features = inputs.shape
    all_cols, spd, blk, _ = gate_blocks.shape
    cols = all_cols // nz
    me = lax.axis_index("narrow")
    z, core = me // 2, me % 2
    wide = lax.axis_index("wide")
    shifts = sorted(range(1, nz), key=lambda r: -min(r, nz - r))

    def along_z(a, s):
        with jax.named_scope(f"along_z{s}"):
            return lax.ppermute(a, "narrow", [(i, (i + 2 * s) % narrow) for i in range(narrow)])

    def swap(a):
        with jax.named_scope("swap"):
            return lax.ppermute(a, "narrow", [(i, i ^ 1) for i in range(narrow)])

    def over_wide(a, m):
        with jax.named_scope(f"wide{m}"):
            return lax.ppermute(a, "wide", [(i, i ^ m) for i in range(nw)])

    where = z.reshape(1).astype(jnp.int32)
    mine = lax.dynamic_slice_in_dim(pattern, cols * z, cols, 0)
    slot_of = jnp.stack(
        [
            ((z - r + nz) % nz * 2 + (core ^ c)) * spd + i
            for r in range(nz)
            for c in range(2)
            for i in range(spd)
        ]
    )
    rows_of = jnp.take(mine, slot_of, axis=1)
    per_device = features // blk
    places = jnp.stack([(rows_of // per_device) ^ wide, rows_of % per_device], axis=-1)

    edges = [cols * k // CHUNKS for k in range(CHUNKS, -1, -1)]
    edges = [cols - e for e in edges]
    chunks = list(zip(edges[:-1], edges[1:]))
    bounds = [(0, 0, cols)] + [(r, lo, hi) for lo, hi in chunks for r in shifts]
    own, *messages = pack_call(nz, bounds, where, gate_blocks, up_blocks, grad_hidden)

    half = tokens // 2
    x_z = {1: along_z(inputs, 1), 3: along_z(inputs, 3)}
    x_z[2] = along_z(x_z[1], 1)
    x_parts, layout = [], []
    for group in ([0], list(range(1, nz))):
        pieces = [inputs if r == 0 else x_z[r] for r in group]
        a, b = (
            jnp.concatenate([p[h * half : (h + 1) * half] for p in pieces], axis=0)
            for h in range(2)
        )
        if x_parts:
            a, b = hold([a, b], *x_parts[-2:], *messages[:1], places)
        n = len(group) * half
        ax, by = over_wide(a, 1), over_wide(b, 2)
        far_a = over_wide(jnp.concatenate([a, ax], axis=0), 2)
        far_b = over_wide(jnp.concatenate([b, by], axis=0), 1)
        x_parts += [a, b, ax, by, far_a, far_b]
        for h, ms in ((0, (0,)), (1, (0,)), (0, (1,)), (1, (2,)), (0, (2, 3)), (1, (1, 3))):
            layout.append(
                tuple(
                    (i * n + k * half, m, r * tokens + h * half, half)
                    for i, m in enumerate(ms)
                    for k, r in enumerate(group)
                )
            )

    earlier = [x_z[2] for r in shifts]
    weights, other = [], None
    for lo, hi in chunks:
        now, messages = messages[: nz - 1], messages[nz - 1 :]
        now = [hold([a], e)[0] for a, e in zip(now, earlier)]
        now = earlier = [along_z(a, r) for a, r in zip(now, shifts)]
        if other is None:
            (own,) = hold([own], *now)
            other = swap(own)
        in_order = [now[shifts.index(r)] for r in range(1, nz)]
        weights.append(([own] + in_order, [other] + [swap(a) for a in in_order]))

    order = [*shifts, 0]
    groups = [[2, 3], [1, 0]]
    columns, sent, parts, back, sums = [], [], [], [], []
    for k, ((lo, hi), (w_own, w_other)) in enumerate(zip(chunks, weights)):
        g_own, g_other, d = forward_call(
            lo, nw, tokens, places[lo:hi], tuple(layout), x_parts, w_own, w_other, sums
        )
        columns.append((w_own, w_other, d))
        if k + 1 < len(chunks):
            beside = weights[k + 1][0][1:]
        else:
            dx = inputs_call(places, nw, tokens, features, columns, groups, [])
            beside = [dx[0][0], *(sent[-1] if sent else [])]
        g_other = swap(*hold([g_other], *beside))
        sums = [(g_own[r].astype(F32) + g_other[r].astype(F32)).astype(BF16) for r in [0, *shifts]]
        now = sums[1:]
        if sent:
            now = [hold([a], e)[0] for a, e in zip(now, sent[-1])]
        sent.append([along_z(a, nz - r) for a, r in zip(now, shifts)])
        parts += [sums[0], *sent[-1]]
        back += [(r, lo, hi) for r in [0, *shifts]]
    hidden, grad_gate, grad_up = unpack_call(nz, back, where, parts, grad_hidden, gate_blocks)

    total, moved, earlier = None, [], sent[0]
    step = [a for a, r in zip(sent[-1], shifts) if 2 * r != nz]
    for group, (to_y, to_x, keep_a, keep_b) in zip(groups, dx):
        to_y, to_x = hold([to_y, to_x], *earlier)
        to_y, to_x = over_wide(to_y, 2), over_wide(to_x, 1)
        near_a, pass_a = (keep_a[i].astype(F32) + to_y[i].astype(F32) for i in range(2))
        near_b, pass_b = (keep_b[i].astype(F32) + to_x[i].astype(F32) for i in range(2))
        pass_a, pass_b = hold([pass_a.astype(BF16), pass_b.astype(BF16)], *step)
        earlier = [pass_a, pass_b]
        pass_a, pass_b = over_wide(pass_a, 1), over_wide(pass_b, 2)
        halves = near_a + pass_a.astype(F32), near_b + pass_b.astype(F32)
        shares = []
        for i, r in enumerate(group):
            shares.append(jnp.concatenate([a[i * half : (i + 1) * half] for a in halves], axis=0))
        if not moved:
            two, three = hold([a.astype(BF16) for a in shares], *sent[-1])
            moved = [along_z(two, nz - 1), along_z(three, nz - 3)]
            step = moved[:1]
        else:
            one = (shares[0] + moved[0].astype(F32)).astype(BF16)
            total = along_z(one, nz - 1).astype(F32) + moved[1].astype(F32) + shares[1]
    return hidden, total.astype(BF16), grad_gate, grad_up


def solution(mesh):
    narrow, nw = mesh.shape["narrow"], mesh.shape["wide"]

    def shards(inputs, gate_blocks, up_blocks, pattern, grad_hidden):
        columns = gate_blocks.shape[0]
        if narrow % 2 == 0 and columns % (narrow // 2) == 0 and narrow == 8 and nw == 4:
            return moved_tokens(
                narrow, nw, inputs, gate_blocks, up_blocks, pattern, grad_hidden
            )
        return gathered_weights(inputs, gate_blocks, up_blocks, pattern, grad_hidden)

    placed = (
        P("narrow", "wide"),
        P("wide", "narrow", None, None),
        P("wide", "narrow", None, None),
        P("wide", None),
        P("narrow", "wide"),
    )
    return jax.shard_map(
        shards,
        mesh=mesh,
        in_specs=placed,
        out_specs=(
            P("narrow", "wide"),
            P("narrow", "wide"),
            P("wide", "narrow", None, None),
            P("wide", "narrow", None, None),
        ),
        check_vma=False,
    )
```

```python
import functools

import jax
import jax.numpy as jnp
from jax import lax
from jax.experimental import pallas as pl
from jax.experimental.pallas import tpu as pltpu
from jax.sharding import PartitionSpec as P


def silu_parts(gate_sum):
    sigmoid_value = jax.nn.sigmoid(gate_sum)
    return (gate_sum * sigmoid_value, sigmoid_value * (1.0 + gate_sum * (1.0 - sigmoid_value)))


def gathered_weights(inputs, gate_blocks, up_blocks, pattern, grad_hidden):
    tokens_here = inputs.shape[0]
    block_size = gate_blocks.shape[2]
    columns = gate_blocks.shape[0]
    full_inputs = lax.all_gather(inputs, "wide", axis=1, tiled=True)
    row_blocks = full_inputs.shape[1] // block_size
    input_blocks = full_inputs.reshape(tokens_here, row_blocks, block_size)
    picked = jnp.take(input_blocks, pattern, axis=1)
    gate_all = lax.all_gather(gate_blocks, "narrow", axis=1, tiled=True)
    up_all = lax.all_gather(up_blocks, "narrow", axis=1, tiled=True)
    gate_sum = jnp.einsum("tjkb,jkbc->tjc", picked, gate_all, preferred_element_type=jnp.float32)
    up_sum = jnp.einsum("tjkb,jkbc->tjc", picked, up_all, preferred_element_type=jnp.float32)
    activation, derivative = silu_parts(gate_sum)
    hidden = (activation * up_sum).astype(jnp.bfloat16)
    cotangent = grad_hidden.reshape(tokens_here, columns, block_size).astype(jnp.float32)
    d_gate = (cotangent * up_sum * derivative).astype(jnp.bfloat16)
    d_up = (cotangent * activation).astype(jnp.bfloat16)
    zero_inputs = jnp.zeros((tokens_here, row_blocks, block_size), jnp.float32)

    def one_slot(k, running):
        gate_slot = lax.dynamic_index_in_dim(gate_all, k, 1, keepdims=False)
        up_slot = lax.dynamic_index_in_dim(up_all, k, 1, keepdims=False)
        contribution = jnp.einsum(
            "tjc,jbc->tjb", d_gate, gate_slot, preferred_element_type=jnp.float32
        )
        contribution = contribution + jnp.einsum(
            "tjc,jbc->tjb", d_up, up_slot, preferred_element_type=jnp.float32
        )
        targets = lax.dynamic_index_in_dim(pattern, k, 1, keepdims=False)
        return running.at[:, targets].add(contribution)

    partial_inputs = lax.fori_loop(0, gate_all.shape[1], one_slot, zero_inputs)
    grad_inputs = lax.psum_scatter(
        partial_inputs.reshape(tokens_here, row_blocks * block_size).astype(jnp.bfloat16),
        "wide",
        scatter_dimension=1,
        tiled=True,
    )
    gate_terms = jnp.einsum("tjkb,tjc->jkbc", picked, d_gate, preferred_element_type=jnp.float32)
    up_terms = jnp.einsum("tjkb,tjc->jkbc", picked, d_up, preferred_element_type=jnp.float32)
    grad_gate = lax.psum_scatter(
        gate_terms.astype(jnp.bfloat16), "narrow", scatter_dimension=1, tiled=True
    )
    grad_up = lax.psum_scatter(
        up_terms.astype(jnp.bfloat16), "narrow", scatter_dimension=1, tiled=True
    )
    return hidden.reshape(tokens_here, columns * block_size), grad_inputs, grad_gate, grad_up


BF16, F32 = jnp.bfloat16, jnp.float32
CHUNKS = 2


ANY = pl.BlockSpec(memory_space=pl.ANY)


def taker(refs):
    refs = list(refs)

    def take(n):
        out = refs[:n]
        del refs[:n]
        return out

    return take


def place_of(places, step, q, blk):
    return places[step, q, 0], pl.multiple_of(places[step, q, 1] * blk, blk)


def forward_kernel(nz, nw, spd, unread, layout, places, *refs):
    take = taker(refs)
    x_in = take(len(layout))
    w_own, w_other = take(nz), take(nz)
    take(unread)
    (g_own, g_other, d_out) = take(nz), take(1)[0], take(1)[0]
    x_all, x_col, w_col, sems = take(4)
    step = pl.program_id(0)
    tokens = d_out.shape[1] // nz
    blk = d_out.shape[-1] // 2
    slots = nz * 2 * spd

    @pl.when(step == 0)
    def _():
        copies = []
        for source, pieces in zip(x_in, layout):
            for at, m, rows, n in pieces:
                target = x_all.at[m, pl.ds(rows, n)]
                sem = sems.at[len(copies)]
                copies.append(pltpu.make_async_copy(source.at[pl.ds(at, n)], target, sem))
        for c in copies:
            c.start()
        for c in copies:
            c.wait()

    for q in range(slots):
        r, i = q // (2 * spd), q % spd
        piece = (w_other if q // spd % 2 else w_own)[r]
        m, at = place_of(places, step, q, blk)
        x_col[:, q * blk : (q + 1) * blk] = x_all[m, :, pl.ds(at, blk)]
        w_col[q * blk : (q + 1) * blk, :blk] = piece[i, 0]
        w_col[q * blk : (q + 1) * blk, blk:] = piece[spd + i, 0]
    both = jnp.dot(x_col[...], w_col[...], preferred_element_type=F32)
    gate, up = both[:, :blk], both[:, blk:]
    activation, derivative = silu_parts(gate)
    hidden = (activation * up).astype(BF16)
    cotangent = jnp.concatenate([w[2 * spd, 0] for w in w_own], axis=0).astype(F32)
    d_out[0, :, :blk] = (cotangent * up * derivative).astype(BF16)
    d_out[0, :, blk:] = (cotangent * activation).astype(BF16)
    for r in range(nz):
        g_own[r][2 * spd, 0] = hidden[r * tokens : (r + 1) * tokens]
        g_other[r, 2 * spd, 0] = jnp.zeros((tokens, blk), BF16)
    for p in range(slots // 2):
        grads = lax.dot_general(
            x_col[:, 2 * p * blk : (2 * p + 2) * blk],
            d_out[0],
            (((0,), (0,)), ((), ())),
            preferred_element_type=F32,
        ).astype(BF16)
        for h in range(2):
            q = 2 * p + h
            r, i = q // (2 * spd), q % spd
            rows = grads[h * blk : (h + 1) * blk]
            target = g_other.at[r] if q // spd % 2 else g_own[r]
            target[i, 0] = rows[:, :blk]
            target[spd + i, 0] = rows[:, blk:]


def forward_call(lo, nw, tokens, places, layout, x_parts, w_own, w_other, earlier):
    nz, features = len(w_own), x_parts[0].shape[1]
    parts, cols, blk, _ = w_own[1].shape
    spd = parts // 2
    rows, slots = nz * tokens, nz * 2 * spd
    own = pl.BlockSpec((parts, 1, blk, blk), lambda j, s: (0, j, 0, 0))
    own0 = pl.BlockSpec((parts, 1, blk, blk), lambda j, s: (0, j + lo, 0, 0))
    other = pl.BlockSpec((2 * spd, 1, blk, blk), lambda j, s: (0, j, 0, 0))
    other0 = pl.BlockSpec((2 * spd, 1, blk, blk), lambda j, s: (0, j + lo, 0, 0))
    every = pl.BlockSpec((nz, parts, 1, blk, blk), lambda j, s: (0, 0, j, 0, 0))
    d_spec = pl.BlockSpec((1, rows, 2 * blk), lambda j, s: (j, 0, 0))
    outs = pl.pallas_call(
        functools.partial(forward_kernel, nz, nw, spd, len(earlier), layout),
        grid_spec=pltpu.PrefetchScalarGridSpec(
            num_scalar_prefetch=1,
            grid=(cols,),
            in_specs=[ANY] * len(x_parts)
            + [own0]
            + [own] * (nz - 1)
            + [other0]
            + [other] * (nz - 1)
            + [ANY] * len(earlier),
            out_specs=[own] * nz + [every, d_spec],
            scratch_shapes=[
                pltpu.VMEM((nw, rows, features), BF16),
                pltpu.VMEM((rows, slots * blk), BF16),
                pltpu.VMEM((slots * blk, 2 * blk), BF16),
                pltpu.SemaphoreType.DMA((sum(len(p) for p in layout),)),
            ],
        ),
        out_shape=[jax.ShapeDtypeStruct(w_own[1].shape, BF16)] * nz
        + [
            jax.ShapeDtypeStruct((nz, *w_own[1].shape), BF16),
            jax.ShapeDtypeStruct((cols, rows, 2 * blk), BF16),
        ],
        compiler_params=pltpu.CompilerParams(
            dimension_semantics=("arbitrary",), vmem_limit_bytes=28 * 1024 * 1024
        ),
        cost_estimate=pl.CostEstimate(
            flops=8 * rows * slots * blk * blk * cols,
            bytes_accessed=10_000_000 + cols * 2_500_000,
            transcendentals=0,
        ),
    )(places, *x_parts, *w_own, *w_other, *earlier)
    return outs[:nz], outs[nz], outs[nz + 1]


OUT_HALVES = ((0, (2, 3)), (1, (1, 3)), (0, (0, 1)), (1, (0, 2)))


def inputs_kernel(nz, spd, counts, groups, unread, places, *refs):
    take = taker(refs)
    chunks = [(take(nz), take(nz), take(1)[0]) for _ in counts]
    take(unread)
    dx_out = [take(len(OUT_HALVES)) for _ in groups]
    dx_all, w_col = take(2)
    step = pl.program_id(0)
    tokens = dx_all.shape[1] // nz
    blk = w_col.shape[-1] // 2
    slots = nz * 2 * spd

    @pl.when(step == 0)
    def _():
        dx_all[...] = jnp.zeros_like(dx_all)

    start = 0
    for count, (w_own, w_other, d_in) in zip(counts, chunks):

        @pl.when((step >= start) & (step < start + count))
        def _(w_own=w_own, w_other=w_other, d_in=d_in):
            for q in range(slots):
                r, i = q // (2 * spd), q % spd
                piece = (w_other if q // spd % 2 else w_own)[r]
                w_col[q * blk : (q + 1) * blk, :blk] = piece[i, 0]
                w_col[q * blk : (q + 1) * blk, blk:] = piece[spd + i, 0]
            for p in range(slots // 2):
                share = lax.dot_general(
                    d_in[0],
                    w_col[2 * p * blk : (2 * p + 2) * blk],
                    (((1,), (1,)), ((), ())),
                    preferred_element_type=F32,
                )
                for h in range(2):
                    m, at = place_of(places, step, 2 * p + h, blk)
                    dx_all[m, :, pl.ds(at, blk)] += share[:, h * blk : (h + 1) * blk]

        start += count

    @pl.when(step == pl.num_programs(0) - 1)
    def _():
        half = tokens // 2
        for group, out in zip(groups, dx_out):
            for ref, (h, ms) in zip(out, OUT_HALVES):
                for i, m in enumerate(ms):
                    for k, r in enumerate(group):
                        rows = dx_all[m, r * tokens + h * half : r * tokens + (h + 1) * half]
                        ref[i, k * half : (k + 1) * half] = rows.astype(BF16)


def inputs_call(places, nw, tokens, features, chunks, groups, earlier):
    nz = len(chunks[0][0])
    parts, _, blk, _ = chunks[0][0][0].shape
    spd = parts // 2
    rows, slots = nz * tokens, nz * 2 * spd
    counts = tuple(c[0][1].shape[1] for c in chunks)
    in_specs, operands, start = [], [], 0
    for count, (w_own, w_other, d) in zip(counts, chunks):

        def at(j, start=start, count=count):
            return jnp.clip(j - start, 0, count - 1)

        block = pl.BlockSpec((2 * spd, 1, blk, blk), lambda j, s, at=at: (0, at(j), 0, 0))
        block0 = pl.BlockSpec(
            (2 * spd, 1, blk, blk), lambda j, s, at=at, start=start: (0, at(j) + start, 0, 0)
        )
        in_specs += ([block0] + [block] * (nz - 1)) * 2
        in_specs += [pl.BlockSpec((1, rows, 2 * blk), lambda j, s, at=at: (at(j), 0, 0))]
        operands += [*w_own, *w_other, d]
        start += count
    in_specs += [ANY] * len(earlier)
    operands += earlier
    shapes = [(2, len(g) * tokens // 2, features) for g in groups for _ in OUT_HALVES]
    outs = pl.pallas_call(
        functools.partial(inputs_kernel, nz, spd, counts, groups, len(earlier)),
        grid_spec=pltpu.PrefetchScalarGridSpec(
            num_scalar_prefetch=1,
            grid=(start,),
            in_specs=in_specs,
            out_specs=[
                pl.BlockSpec(s, lambda j, s_: (0, 0, 0), pipeline_mode=pl.Buffered(1)) for s in shapes
            ],
            scratch_shapes=[
                pltpu.VMEM((nw, rows, features), F32),
                pltpu.VMEM((slots * blk, 2 * blk), BF16),
            ],
        ),
        out_shape=[jax.ShapeDtypeStruct(s, BF16) for s in shapes],
        compiler_params=pltpu.CompilerParams(
            dimension_semantics=("arbitrary",), vmem_limit_bytes=40 * 1024 * 1024
        ),
        cost_estimate=pl.CostEstimate(
            flops=4 * rows * slots * blk * blk * start,
            bytes_accessed=20_000_000,
            transcendentals=0,
        ),
    )(places, *operands)
    n = len(OUT_HALVES)
    return [outs[g * n : (g + 1) * n] for g in range(len(groups))]


def hold(values, *earlier):
    n = len(values)
    return pl.pallas_call(
        lambda *refs: None,
        in_specs=[ANY] * (n + len(earlier)),
        out_specs=[ANY] * n,
        out_shape=[jax.ShapeDtypeStruct(v.shape, v.dtype) for v in values],
        input_output_aliases={i: i for i in range(n)},
    )(*values, *earlier)


VMEM = pl.BlockSpec(memory_space=pltpu.VMEM)
SMEM = pl.BlockSpec(memory_space=pltpu.SMEM)


def message_blocks(nz, cols, spd, blk, bounds, where):
    for k, (r, lo, hi) in enumerate(bounds):
        first = lax.rem(where[0] + r, nz) * cols + lo
        for j in range(hi - lo):
            yield k, j, first + j, pl.ds(pl.multiple_of((first + j) * blk, blk), blk)


def pack_kernel(nz, cols, spd, bounds, where, gate, up, cot, *outs):
    for k, j, col, at in message_blocks(nz, cols, spd, gate.shape[-1], bounds, where):
        for i in range(spd):
            outs[k][i, j] = gate[col, i]
            outs[k][spd + i, j] = up[col, i]
        outs[k][2 * spd, j] = cot[:, at]


def pack_call(nz, bounds, where, gate, up, cot):
    all_cols, spd, blk, _ = gate.shape
    cols = all_cols // nz
    return pl.pallas_call(
        functools.partial(pack_kernel, nz, cols, spd, bounds),
        in_specs=[SMEM] + [VMEM] * 3,
        out_specs=[VMEM] * len(bounds),
        out_shape=[
            jax.ShapeDtypeStruct((2 * spd + 1, hi - lo, blk, blk), BF16) for _, lo, hi in bounds
        ],
        compiler_params=pltpu.CompilerParams(vmem_limit_bytes=20 * 1024 * 1024),
        cost_estimate=pl.CostEstimate(flops=0, bytes_accessed=10_000_000, transcendentals=0),
    )(where, gate, up, cot)


def unpack_kernel(nz, cols, spd, bounds, where, *refs):
    parts = refs[: len(bounds)]
    hidden, gate, up = refs[len(bounds) :]
    for k, j, col, at in message_blocks(nz, cols, spd, gate.shape[-1], bounds, where):
        for i in range(spd):
            gate[col, i] = parts[k][i, j]
            up[col, i] = parts[k][spd + i, j]
        hidden[:, at] = parts[k][2 * spd, j]


def unpack_call(nz, bounds, where, parts, hidden, gate):
    all_cols, spd, blk, _ = gate.shape
    cols = all_cols // nz
    return pl.pallas_call(
        functools.partial(unpack_kernel, nz, cols, spd, bounds),
        in_specs=[SMEM] + [VMEM] * len(bounds),
        out_specs=[VMEM] * 3,
        out_shape=[jax.ShapeDtypeStruct(a.shape, BF16) for a in (hidden, gate, gate)],
        compiler_params=pltpu.CompilerParams(vmem_limit_bytes=20 * 1024 * 1024),
        cost_estimate=pl.CostEstimate(flops=0, bytes_accessed=10_000_000, transcendentals=0),
    )(where, *parts)


def moved_tokens(narrow, nw, inputs, gate_blocks, up_blocks, pattern, grad_hidden):
    nz = narrow // 2
    tokens, features = inputs.shape
    all_cols, spd, blk, _ = gate_blocks.shape
    cols = all_cols // nz
    me = lax.axis_index("narrow")
    z, core = me // 2, me % 2
    wide = lax.axis_index("wide")
    shifts = sorted(range(1, nz), key=lambda r: -min(r, nz - r))

    def along_z(a, s):
        with jax.named_scope(f"along_z{s}"):
            return lax.ppermute(a, "narrow", [(i, (i + 2 * s) % narrow) for i in range(narrow)])

    def swap(a):
        with jax.named_scope("swap"):
            return lax.ppermute(a, "narrow", [(i, i ^ 1) for i in range(narrow)])

    def over_wide(a, m):
        with jax.named_scope(f"wide{m}"):
            return lax.ppermute(a, "wide", [(i, i ^ m) for i in range(nw)])

    where = z.reshape(1).astype(jnp.int32)
    mine = lax.dynamic_slice_in_dim(pattern, cols * z, cols, 0)
    slot_of = jnp.stack(
        [
            ((z - r + nz) % nz * 2 + (core ^ c)) * spd + i
            for r in range(nz)
            for c in range(2)
            for i in range(spd)
        ]
    )
    rows_of = jnp.take(mine, slot_of, axis=1)
    per_device = features // blk
    places = jnp.stack([(rows_of // per_device) ^ wide, rows_of % per_device], axis=-1)

    edges = [cols * k // CHUNKS for k in range(CHUNKS, -1, -1)]
    edges = [cols - e for e in edges]
    chunks = list(zip(edges[:-1], edges[1:]))
    bounds = [(0, 0, cols)] + [(r, lo, hi) for lo, hi in chunks for r in shifts]
    own, *messages = pack_call(nz, bounds, where, gate_blocks, up_blocks, grad_hidden)

    half = tokens // 2
    x_z = {1: along_z(inputs, 1), 3: along_z(inputs, 3)}
    x_z[2] = along_z(x_z[1], 1)
    x_parts, layout = [], []
    for group in ([0], list(range(1, nz))):
        pieces = [inputs if r == 0 else x_z[r] for r in group]
        a, b = (
            jnp.concatenate([p[h * half : (h + 1) * half] for p in pieces], axis=0)
            for h in range(2)
        )
        if x_parts:
            a, b = hold([a, b], *x_parts[-2:], *messages[:1], places)
        n = len(group) * half
        ax, by = over_wide(a, 1), over_wide(b, 2)
        far_a = over_wide(jnp.concatenate([a, ax], axis=0), 2)
        far_b = over_wide(jnp.concatenate([b, by], axis=0), 1)
        x_parts += [a, b, ax, by, far_a, far_b]
        for h, ms in ((0, (0,)), (1, (0,)), (0, (1,)), (1, (2,)), (0, (2, 3)), (1, (1, 3))):
            layout.append(
                tuple(
                    (i * n + k * half, m, r * tokens + h * half, half)
                    for i, m in enumerate(ms)
                    for k, r in enumerate(group)
                )
            )

    earlier = [x_z[2] for r in shifts]
    weights, other = [], None
    for lo, hi in chunks:
        now, messages = messages[: nz - 1], messages[nz - 1 :]
        now = [hold([a], e)[0] for a, e in zip(now, earlier)]
        now = earlier = [along_z(a, r) for a, r in zip(now, shifts)]
        if other is None:
            (own,) = hold([own], *now)
            other = swap(own)
        in_order = [now[shifts.index(r)] for r in range(1, nz)]
        weights.append(([own] + in_order, [other] + [swap(a) for a in in_order]))

    order = [*shifts, 0]
    groups = [[2, 3], [1, 0]]
    columns, sent, parts, back, sums = [], [], [], [], []
    for k, ((lo, hi), (w_own, w_other)) in enumerate(zip(chunks, weights)):
        g_own, g_other, d = forward_call(
            lo, nw, tokens, places[lo:hi], tuple(layout), x_parts, w_own, w_other, sums
        )
        columns.append((w_own, w_other, d))
        if k + 1 < len(chunks):
            beside = weights[k + 1][0][1:]
        else:
            dx = inputs_call(places, nw, tokens, features, columns, groups, [])
            beside = [dx[0][0], *(sent[-1] if sent else [])]
        g_other = swap(*hold([g_other], *beside))
        sums = [(g_own[r].astype(F32) + g_other[r].astype(F32)).astype(BF16) for r in [0, *shifts]]
        now = sums[1:]
        if sent:
            now = [hold([a], e)[0] for a, e in zip(now, sent[-1])]
        sent.append([along_z(a, nz - r) for a, r in zip(now, shifts)])
        parts += [sums[0], *sent[-1]]
        back += [(r, lo, hi) for r in [0, *shifts]]
    hidden, grad_gate, grad_up = unpack_call(nz, back, where, parts, grad_hidden, gate_blocks)

    total, moved, earlier = None, [], sent[0]
    step = [a for a, r in zip(sent[-1], shifts) if 2 * r != nz]
    for group, (to_y, to_x, keep_a, keep_b) in zip(groups, dx):
        to_y, to_x = hold([to_y, to_x], *earlier)
        to_y, to_x = over_wide(to_y, 2), over_wide(to_x, 1)
        near_a, pass_a = (keep_a[i].astype(F32) + to_y[i].astype(F32) for i in range(2))
        near_b, pass_b = (keep_b[i].astype(F32) + to_x[i].astype(F32) for i in range(2))
        pass_a, pass_b = hold([pass_a.astype(BF16), pass_b.astype(BF16)], *step)
        earlier = [pass_a, pass_b]
        pass_a, pass_b = over_wide(pass_a, 1), over_wide(pass_b, 2)
        halves = near_a + pass_a.astype(F32), near_b + pass_b.astype(F32)
        shares = []
        for i, r in enumerate(group):
            shares.append(jnp.concatenate([a[i * half : (i + 1) * half] for a in halves], axis=0))
        if not moved:
            two, three = hold([a.astype(BF16) for a in shares], *sent[-1])
            moved = [along_z(two, nz - 1), along_z(three, nz - 3)]
            step = moved[1:]
        else:
            one = (shares[0] + moved[0].astype(F32)).astype(BF16)
            total = along_z(one, nz - 1).astype(F32) + moved[1].astype(F32) + shares[1]
    return hidden, total.astype(BF16), grad_gate, grad_up


def solution(mesh):
    narrow, nw = mesh.shape["narrow"], mesh.shape["wide"]

    def shards(inputs, gate_blocks, up_blocks, pattern, grad_hidden):
        columns = gate_blocks.shape[0]
        if narrow % 2 == 0 and columns % (narrow // 2) == 0 and narrow == 8 and nw == 4:
            return moved_tokens(
                narrow, nw, inputs, gate_blocks, up_blocks, pattern, grad_hidden
            )
        return gathered_weights(inputs, gate_blocks, up_blocks, pattern, grad_hidden)

    placed = (
        P("narrow", "wide"),
        P("wide", "narrow", None, None),
        P("wide", "narrow", None, None),
        P("wide", None),
        P("narrow", "wide"),
    )
    return jax.shard_map(
        shards,
        mesh=mesh,
        in_specs=placed,
        out_specs=(
            P("narrow", "wide"),
            P("narrow", "wide"),
            P("wide", "narrow", None, None),
            P("wide", "narrow", None, None),
        ),
        check_vma=False,
    )
```
